256 devices in a mesh: dp: 32 (over y_lo, z, core), mp: 8 (over x, y_hi).
Axes of the slice: x: 4, y: 4 (y_hi: 2, y_lo: 2; y = y_hi * 2 + y_lo), z: 8, core: 2. Of those that a mesh axis runs over, the one named last changes fastest.
Arguments:
- activations: bfloat16 [4096, 3584], P('dp'), may hold values from -6 to 6
- out_grads: bfloat16 [4096, 16384], P('dp', 'mp'), may hold values from -0.00390625 to 0.00390625
- slot_blocks: int32 [8, 32], replicated, may hold values from 0 to 31, as said below
- refresh_ids: int32 [8, 7], replicated, may hold values from 0 to 27, as said below
- left_stats: float32 [8, 32, 512, 512], P('mp', 'dp'), may hold values from -4 to 52, as said below
- right_stats: float32 [8, 32, 512, 512], P('mp', 'dp'), may hold values from -4 to 52, as said below
- left_roots: float32 [8, 32, 512, 512], P('mp', 'dp'), may hold values from -2 to 18, as said below
- right_roots: float32 [8, 32, 512, 512], P('mp', 'dp'), may hold values from -2 to 18, as said below
- weight_blocks: bfloat16 [8, 32, 512, 512], P('mp', 'dp'), may hold values from -0.09375 to 0.09375
Outputs:
- new_left: float32 [8, 32, 512, 512], P('mp', 'dp')
- new_right: float32 [8, 32, 512, 512], P('mp', 'dp')
- new_left_roots: float32 [8, 32, 512, 512], P('mp', 'dp')
- new_right_roots: float32 [8, 32, 512, 512], P('mp', 'dp')
- new_weights: bfloat16 [8, 32, 512, 512], P('mp', 'dp')
- projected: bfloat16 [4096, 16384], P('dp', 'mp')
The draws below stay inside these ranges and needn't reach their ends.
Inputs may be any that keep to these rules, and one draw needn't show every extreme that they name: `slot_blocks`: each row is a permutation of 0 to 31; slot s belongs to dp index s; a value of 28 or more marks an empty slot. `refresh_ids`: each row holds 7 distinct blocks of that mp index. For every slot s and every k, at most one of the blocks held at slot s by mp indices 2 k and 2 k + 1 is listed. `left_stats`: every block is symmetric positive definite. `right_stats`: every block is symmetric positive definite. `left_roots`: every block is symmetric positive definite. `right_roots`: every block is symmetric positive definite.
All inputs are finite; a program needn't handle non-finite values.
Results may differ from the reference program's by a relative error of at most 0.0043.
Values may be sent and summed in bfloat16 or wider, within the bound.
A program may use at most 128 MiB of HBM per device.

```python
import math
import jax
import jax.numpy as jnp
from jax import lax

BS = 512
D_WIN = 3584
FF_DEV = 2048
ITERS = 3
RB = 7
CB = 4
NBLK = 28
SLOTS = 32
QUART = 7
TOKENS = 4096
FF_WIN = 16384
N_MP = 8


def plan_tables(key):
    first, second = jax.random.split(key)
    slot_table = jax.vmap(lambda sub: jax.random.permutation(sub, SLOTS))(jax.random.split(first, N_MP)).astype(jnp.int32)
    ranks = jax.vmap(lambda sub: jax.random.permutation(sub, SLOTS))(jax.random.split(second, N_MP)).astype(jnp.int32)
    empty = (slot_table >= NBLK).astype(jnp.int32)
    topmost = (slot_table[0::2] == NBLK - 1).astype(jnp.int32)
    score_upper = ranks[0::2] + SLOTS * empty[0::2] - (SLOTS + 1) * topmost
    pick_upper = jnp.argsort(score_upper, axis=1, stable=True)[:, :QUART]
    taken = jax.vmap(lambda picks: jnp.zeros((SLOTS,), jnp.int32).at[picks].set(1))(pick_upper)
    score_lower = ranks[1::2] + SLOTS * jnp.maximum(empty[1::2], taken)
    pick_lower = jnp.argsort(score_lower, axis=1, stable=True)[:, :QUART]
    ids_upper = jnp.take_along_axis(slot_table[0::2], pick_upper, axis=1)
    ids_lower = jnp.take_along_axis(slot_table[1::2], pick_lower, axis=1)
    refresh = jnp.stack([ids_upper, ids_lower], axis=1).reshape(N_MP, QUART)
    return (slot_table, refresh.astype(jnp.int32))


def spd_blocks(key, top, factor):
    first, second, third = jax.random.split(key, 3)
    scales = jnp.exp(jax.random.uniform(first, (N_MP, SLOTS, BS), jnp.float32, 0.0, math.log(top)))
    diagonal = jax.random.uniform(second, (N_MP, SLOTS, BS), jnp.float32, 1.6, 3.2)
    noise = jax.random.uniform(third, (N_MP, SLOTS, BS, BS), jnp.float32, -1.25, 1.25) / math.sqrt(BS)
    ident = jnp.eye(BS, dtype=jnp.float32)
    offdiag = 0.5 * (noise + jnp.swapaxes(noise, 2, 3)) * (1.0 - ident)
    matrix = offdiag + diagonal[..., None] * ident
    return factor * scales[..., :, None] * matrix * scales[..., None, :]


def draw_slot_blocks(key, part):
    return plan_tables(key)[0]


def draw_refresh_ids(key, part):
    return plan_tables(key)[1]


def draw_left_stats(key, part):
    key = jax.random.fold_in(key, 11)
    top = 3.0
    return spd_blocks(key, top, 1.0)


def draw_right_stats(key, part):
    key = jax.random.fold_in(key, 12)
    top = 3.0
    return spd_blocks(key, top, 1.0)


def draw_left_roots(key, part):
    key = jax.random.fold_in(key, 13)
    top = 3.0
    return spd_blocks(key, top, 0.35)


def draw_right_roots(key, part):
    key = jax.random.fold_in(key, 14)
    top = 3.0
    return spd_blocks(key, top, 0.35)


def shard_levels(rng, dims, shards, least, largest):
    def one(position, blocks):
        steps = jax.random.uniform(jax.random.fold_in(jax.random.fold_in(rng, 6), position), (blocks,), jnp.float32, least / len(shards), largest / len(shards))
        return jnp.repeat(jnp.exp(steps), dims[position] // blocks).reshape((-1,) + (1,) * (len(dims) - position - 1))

    loudness = one(*shards[0])
    for cut in shards[1:]:
        loudness = loudness * one(*cut)
    return loudness


def centred(key, shape, width, reach, cuts=(), held_as=jnp.bfloat16):
    drawn = jax.random.normal(key, shape, jnp.float32) * width
    if len(cuts) > 0:
        drawn = shard_levels(key, shape, cuts, -0.22, 0.18) * drawn
    return jnp.clip(drawn, min=-reach, max=reach).astype(held_as)


def setup_inputs(seed: int = 0) -> dict:
    keys = jax.random.split(jax.random.key(seed), 10)
    return {
        "activations": centred(keys[0], (TOKENS, D_WIN), 1.0, 6.0, ((0, 32),)),
        "out_grads": centred(keys[1], (TOKENS, FF_WIN), (TOKENS * BS) ** -0.5, 0.00390625, ((0, 32), (1, 8))),
        "slot_blocks": draw_slot_blocks(jax.random.fold_in(keys[9], 71), 0),
        "refresh_ids": draw_refresh_ids(jax.random.fold_in(keys[9], 71), 0),
        "left_stats": draw_left_stats(jax.random.fold_in(keys[9], 71), 0),
        "right_stats": draw_right_stats(jax.random.fold_in(keys[9], 71), 0),
        "left_roots": draw_left_roots(jax.random.fold_in(keys[9], 71), 0),
        "right_roots": draw_right_roots(jax.random.fold_in(keys[9], 71), 0),
        "weight_blocks": centred(keys[8], (N_MP, SLOTS, BS, BS), D_WIN ** -0.5, 0.09375, ((0, 8), (1, 32))),
    }


BETA = 0.9
STEP = 0.1
EPS = 1e-06

def mat(left, right):
    return jnp.matmul(left, right, precision=lax.Precision.HIGHEST)

def root_newton(stats):
    total = jnp.sum(stats * stats)
    scale = 5.0 / (2.0 * jnp.sqrt(total + EPS))
    ident = jnp.eye(stats.shape[-1], dtype=jnp.float32)
    iterate = jnp.power(scale, 0.25) * ident
    coupled = scale * stats
    for step in range(ITERS):
        factor = (5.0 * ident - coupled) / 4.0
        iterate = mat(iterate, factor)
        square = mat(factor, factor)
        coupled = mat(mat(square, square), coupled)
    return iterate

def reference(activations, out_grads, slot_blocks, refresh_ids, left_stats, right_stats, left_roots, right_roots, weight_blocks):
    feats = activations.reshape(TOKENS, RB, BS)
    grads4 = out_grads.reshape(TOKENS, N_MP, CB, BS)
    flags = jnp.any(slot_blocks[:, :, None] == refresh_ids[:, None, :], axis=2) & (slot_blocks < NBLK)
    mp_index = jnp.repeat(jnp.arange(N_MP, dtype=jnp.int32), SLOTS)

    def one_slot(item):
        mp_row, block, flag, left, right, lroot, rroot, wblock = item
        filled = block < NBLK
        safe = jnp.where(filled, block, 0).astype(jnp.int32)
        row_block = safe // CB
        col_block = safe % CB
        feat_cols = lax.dynamic_index_in_dim(feats, row_block, 1, keepdims=False)
        grad_cols = grads4[:, mp_row, col_block, :]
        grad = jnp.dot(feat_cols.T, grad_cols, preferred_element_type=jnp.float32)
        grad = grad * filled.astype(jnp.float32)
        new_l = BETA * left + mat(grad, grad.T)
        new_r = BETA * right + mat(grad.T, grad)
        update = mat(mat(lroot, grad), rroot)
        new_w = (wblock.astype(jnp.float32) - STEP * update).astype(jnp.bfloat16)
        roots = lax.cond(flag, lambda: (root_newton(new_l), root_newton(new_r)), lambda: (lroot, rroot))
        return (new_l, new_r, roots[0], roots[1], new_w)
    square_shape = (N_MP * SLOTS, BS, BS)
    outs = lax.map(one_slot, (mp_index, slot_blocks.reshape(-1), flags.reshape(-1), left_stats.reshape(square_shape), right_stats.reshape(square_shape), left_roots.reshape(square_shape), right_roots.reshape(square_shape), weight_blocks.reshape(square_shape)))
    full_shape = (N_MP, SLOTS, BS, BS)
    new_left = outs[0].reshape(full_shape)
    new_right = outs[1].reshape(full_shape)
    new_left_roots = outs[2].reshape(full_shape)
    new_right_roots = outs[3].reshape(full_shape)
    new_weights = outs[4].reshape(full_shape)
    columns = []
    for mp_row in range(N_MP):
        order = jnp.argsort(slot_blocks[mp_row], stable=True)
        chosen = new_weights[mp_row][order[:NBLK]]
        full = chosen.reshape(RB, CB, BS, BS).transpose(0, 2, 1, 3).reshape(D_WIN, FF_DEV)
        columns.append(jnp.dot(activations, full, preferred_element_type=jnp.float32))
    projected = jnp.concatenate(columns, axis=1).astype(jnp.bfloat16)
    return (new_left, new_right, new_left_roots, new_right_roots, new_weights, projected)
```

```python
import functools

import jax
import jax.numpy as jnp
from jax import lax
from jax.experimental import pallas as pl
from jax.experimental.pallas import tpu as pltpu
from jax.sharding import PartitionSpec as P

BETA = 0.9
STEP = 0.1
EPS = 1e-06
CB = 4

MESH = pl.DeviceIdType.MESH
BF = jnp.bfloat16
F32 = jnp.float32


def dot(left, right):
    return jnp.dot(left, right, preferred_element_type=F32)


def dot_tn(left, right):
    return lax.dot_general(left, right, (((0,), (0,)), ((), ())), preferred_element_type=F32)


def dot_nt(left, right):
    return lax.dot_general(left, right, (((1,), (1,)), ((), ())), preferred_element_type=F32)


def split(value):
    high = value.astype(BF)
    return high, (value - high.astype(F32)).astype(BF)


def kernel(
    zs, toks, rb, bs, slots,
    table, plan, act, og, ls, rs, lr, rr, wb,
    nl_out, nr_out, lroot_out, rroot_out, nw_out, proj_out,
    a_lo, a_hi, e_all, far_s, far_r, near_s, near_r, wag, acc, ysend, yrecv, pout,
    nl, nr, lold, rold, wold, lh, ll, rh, rl, gh, gl, th, tl,
    nf, m1f, xf, mb0, mb1, nb, kb, xb,
    load_sem, p0_send, p0_recv, rs_send, rs_recv, ag_send, ag_recv, sib_send, sib_recv, y_ssem, y_rsem, store_sem,
):
    half = bs // 2
    quarter = bs // 4
    far = zs // 2
    nblk = rb * CB
    dp = lax.axis_index("dp")
    mp = lax.axis_index("mp")
    core = lax.rem(dp, 2)
    z = lax.rem(dp // 2, zs)
    y = dp // (2 * zs)

    def device(yy, zz, cc):
        return yy * (2 * zs) + zz * 2 + cc

    up = lax.rem(z + 1, zs)
    down = lax.rem(z + zs - 1, zs)
    ring = ((device(y, up, core), mp), (device(y, down, core), mp))
    sibling = (device(y, z, 1 - core), mp)
    across = (device(1 - y, z, core), mp)
    across_other = (device(1 - y, z, core), mp + 1 - 2 * lax.rem(mp, 2))

    def remote(src, dst, send, recv, to):
        copy = pltpu.make_async_remote_copy(
            src_ref=src, dst_ref=dst, send_sem=send, recv_sem=recv, device_id=to, device_id_type=MESH
        )
        copy.start()
        return copy

    def rows_of(yy, cc):
        return pl.ds(pl.multiple_of((cc * 2 + yy) * toks, toks), toks)

    def local(src, dst, sem):
        copy = pltpu.make_async_copy(src, dst, sem)
        copy.start()
        return copy

    mine = rows_of(y, core)
    loads_e = [local(og.at[:, k * bs : (k + 1) * bs], e_all.at[k, mine, :], load_sem.at[k]) for k in range(CB)]
    loads_a = []
    for h, dst in enumerate((a_lo, a_hi)):
        for r in range(rb):
            lo = r * bs + h * half
            loads_a.append(local(act.at[:, lo : lo + half], dst.at[r, mine, :], load_sem.at[CB + h * rb + r]))
    base = CB + 2 * rb
    load_mats = [
        local(src, dst, load_sem.at[base + k])
        for k, (src, dst) in enumerate(((lr, lold), (rr, rold), (wb, wold), (ls, nl), (rs, nr)))
    ]

    barrier = pltpu.get_barrier_semaphore()
    for other in (sibling, across, across_other) + ring:
        pl.semaphore_signal(barrier, inc=1, device_id=other, device_id_type=MESH)
    pl.semaphore_wait(barrier, 5)

    def part(number, rows):
        if number == 0:
            return e_all.at[:, rows, :]
        if number == 1:
            return a_lo.at[:, rows, :]
        if number == 2:
            return a_hi.at[rb - 2 : rb, rows, :]
        return a_hi.at[0 : rb - 2, rows, :]

    def send_part(number, rows, slot, to):
        ref = part(number, rows)
        return remote(ref, ref, p0_send.at[slot], p0_recv.at[slot], to)

    for copy in loads_e:
        copy.wait()
    outgoing = [send_part(0, mine, 0, across)]
    own_to_sibling = [send_part(0, mine, 4, sibling)]
    for copy in loads_a:
        copy.wait()
    outgoing.append(send_part(1, mine, 1, across_other))
    own_to_sibling.append(send_part(1, mine, 5, sibling))
    outgoing.append(send_part(2, mine, 2, across))
    outgoing.append(send_part(3, mine, 3, across_other))
    own_to_sibling.append(send_part(2, mine, 6, sibling))
    own_to_sibling.append(send_part(3, mine, 7, sibling))
    theirs = rows_of(1 - y, core)
    forwarded = []
    for number in (0, 1, 2, 3):
        outgoing[number].wait_recv()
        forwarded.append(send_part(number, theirs, 8 + number, sibling))

    for copy in load_mats:
        copy.wait()
    lh[...], ll[...] = split(lold[...])
    rh[...], rl[...] = split(rold[...])

    def block_at(zz, cc):
        return table[mp, y * (2 * zs) + zz * 2 + cc]

    def row_and_col(block):
        safe = jnp.where(block < nblk, block, 0)
        return safe // CB, lax.rem(safe, CB)

    def partial_grad(zz, i):
        r, c = row_and_col(block_at(zz, core))
        return dot_tn((a_lo, a_hi)[i][r], e_all[c])

    far_copy = {}
    near_copy = {}
    for i in range(2):
        if i == 0:
            for number in (0, 1):
                own_to_sibling[number].wait_recv()
                forwarded[number].wait_recv()
        else:
            for number in (2, 3):
                own_to_sibling[number].wait_recv()
                forwarded[number].wait_recv()
        value = partial_grad(lax.rem(z + far, zs), i).astype(BF)
        for way in range(2):
            far_s[way, i] = value[:, way * half : (way + 1) * half]
            far_copy[way, i] = remote(
                far_s.at[way, i], far_r.at[way, i], rs_send.at[way, 0, i], rs_recv.at[way, 0, i], ring[way]
            )
    for d in range(far - 1, 0, -1):
        for i in range(2):
            for way in range(2):
                zz = lax.rem(z + d, zs) if way == 0 else lax.rem(z + zs - d, zs)
                value = partial_grad(zz, i)
                if d == far - 1:
                    cols = slice(way * half, (way + 1) * half)
                    rest = slice((1 - way) * half, (2 - way) * half)
                    near_s[way, d - 1, i, :, rest] = value[:, rest].astype(BF)
                    far_copy[way, i].wait_recv()
                    near_s[way, d - 1, i, :, cols] = (value[:, cols] + far_r[way, i].astype(F32)).astype(BF)
                else:
                    near_copy[way, d + 1, i].wait_recv()
                    near_s[way, d - 1, i] = (value + near_r[way, d, i].astype(F32)).astype(BF)
                near_copy[way, d, i] = remote(
                    near_s.at[way, d - 1, i],
                    near_r.at[way, d - 1, i],
                    rs_send.at[way, d, i],
                    rs_recv.at[way, d, i],
                    ring[way],
                )
    own_block = block_at(z, core)
    filled = jnp.where(own_block < nblk, 1.0, 0.0).astype(F32)
    total = None
    for i in range(2):
        rows = slice(i * half, (i + 1) * half)
        value = partial_grad(z, i)
        near_copy[0, 1, i].wait_recv()
        near_copy[1, 1, i].wait_recv()
        value = (value + near_r[0, 0, i].astype(F32) + near_r[1, 0, i].astype(F32)) * filled
        high, low = split(value)
        gh[rows, :] = high
        gl[rows, :] = low
        term = dot(lh[:, rows], high) + dot(lh[:, rows], low) + dot(ll[:, rows], high)
        total = term if total is None else total + term
    th[...], tl[...] = split(total)

    stores = []
    ag = {}
    sib = {}

    def piece(cc, zz, p, k):
        return wag.at[cc, zz, p, :, k * quarter : (k + 1) * quarter]

    def send_ring(way, zz, d, p, k):
        ref = piece(core, zz, p, k)
        ag[way, d, p, k] = remote(ref, ref, ag_send.at[way, d - 1, p, k], ag_recv.at[way, d - 1, p, k], ring[way])

    def send_sibling(zz, step, p):
        ref = wag.at[core, zz, p]
        sib[step, p] = remote(ref, ref, sib_send.at[step, p], sib_recv.at[step, p], sibling)

    def reach(way, k):
        return far if way == k else far - 1

    def behind(way, d):
        return lax.rem(z + zs - d, zs) if way == 0 else lax.rem(z + d, zs)

    def make_weights(p):
        cols = slice(p * half, (p + 1) * half)
        update = dot(th[...], rh[:, cols]) + dot(th[...], rl[:, cols]) + dot(tl[...], rh[:, cols])
        wag[core, z, p] = (wold[:, cols].astype(F32) - STEP * update).astype(BF)

    def send_own(p):
        for k in range(2):
            for way in range(2):
                order = k if way == 0 else 1 - k
                send_ring(way, z, 1, p, order)
        send_sibling(z, 0, p)
        stores.append(local(wag.at[core, z, p], nw_out.at[:, p * half : (p + 1) * half], store_sem.at[p]))

    def add_products(p, items):
        lo, hi = p * half, (p + 1) * half
        terms = []
        for cc, zz in items:
            block = block_at(zz, cc)
            r, c = row_and_col(block)
            rows = pl.ds(pl.multiple_of(core * (2 * toks), 2 * toks), 2 * toks)
            term = dot(a_lo[r, rows, :], wag[cc, zz, p, 0:half, :]) + dot(a_hi[r, rows, :], wag[cc, zz, p, half:bs, :])
            terms.append((block, c, term))
        for col in range(CB):
            value = acc[col, :, lo:hi]
            for block, c, term in terms:
                weight = jnp.where((block < nblk) & (c == col), 1.0, 0.0).astype(F32)
                value = value + term * weight
            acc[col, :, lo:hi] = value

    own_flag = jnp.zeros((), jnp.int32)
    for k in range(plan.shape[1]):
        own_flag = jnp.where(plan[mp, k] == own_block, 1, own_flag)
    own_flag = jnp.where(own_block < nblk, own_flag, 0)

    def new_left():
        nl[...] = BETA * nl[...] + dot_nt(gh[...], gh[...]) + dot_nt(gh[...], gl[...]) + dot_nt(gl[...], gh[...])
        stores.append(local(nl, nl_out, store_sem.at[2]))

    def new_right():
        nr[...] = BETA * nr[...] + dot_tn(gh[...], gh[...]) + dot_tn(gh[...], gl[...]) + dot_tn(gl[...], gh[...])
        stores.append(local(nr, nr_out, store_sem.at[3]))

    width = half

    def eye_tile(lo):
        rows = lax.broadcasted_iota(jnp.int32, (bs, width), 0)
        cols = lax.broadcasted_iota(jnp.int32, (bs, width), 1) + lo
        return jnp.where(rows == cols, 1.0, 0.0).astype(F32)

    def tiles(body):
        for lo in range(0, bs, width):
            body(slice(lo, lo + width), lo)

    def newton(stats, old, out, number):
        scale = {}

        def start():
            total = jnp.sum(stats[...] * stats[...], axis=(0, 1), keepdims=True)
            scale["z"] = 5.0 / (2.0 * jnp.sqrt(total + EPS))
            scale["root"] = jnp.sqrt(jnp.sqrt(scale["z"]))
            mb0[...] = (scale["z"] * stats[...]).astype(BF)

            def body(cols, lo):
                value = (-0.625 * scale["z"]) * stats[:, cols] + 0.0625 * dot(mb0[...], mb0[:, cols])
                nf[:, cols] = value
                nb[:, cols] = value.astype(BF)

            tiles(body)

        def fourth_power():
            def body(cols, lo):
                kb[:, cols] = (3.125 * nf[:, cols] + dot(nb[...], nb[:, cols])).astype(BF)

            tiles(body)

        def first_coupled():
            def body(cols, lo):
                value = (2.44140625 * scale["z"]) * stats[:, cols] + dot(kb[...], mb0[:, cols])
                m1f[:, cols] = value
                mb1[:, cols] = value.astype(BF)

            tiles(body)

        def second_iterate():
            def body(cols, lo):
                value = 1.5625 * eye_tile(lo) - 0.3125 * (scale["z"] * stats[:, cols] + m1f[:, cols])
                value = scale["root"] * (value + 0.0625 * dot(mb0[...], mb1[:, cols]))
                xf[:, cols] = value
                xb[:, cols] = value.astype(BF)

            tiles(body)

        def second_square():
            def body(cols, lo):
                value = -0.625 * m1f[:, cols] + 0.0625 * dot(mb1[...], mb1[:, cols])
                nf[:, cols] = value
                nb[:, cols] = value.astype(BF)

            tiles(body)

        def second_coupled():
            def body(cols, lo):
                mb0[:, cols] = (2.44140625 * m1f[:, cols] + dot(kb[...], mb1[:, cols])).astype(BF)

            tiles(body)

        def finish():
            mask = jnp.full((bs, width), own_flag, jnp.int32) > 0

            def body(cols, lo):
                value = 1.25 * xf[:, cols] - 0.25 * dot(xb[...], mb0[:, cols])
                old[:, cols] = jnp.where(mask, value, old[:, cols])

            tiles(body)
            stores.append(local(old, out, store_sem.at[number]))

        return [start, fourth_power, first_coupled, second_iterate, second_square, fourth_power, second_coupled, finish]

    work = [new_left, new_right] + newton(nl, lold, lroot_out, 4) + newton(nr, rold, rroot_out, 5)

    def some(count):
        for _ in range(count):
            if work:
                work.pop(0)()

    def projection_part(p):
        other = pl.ds(pl.multiple_of((1 - y) * toks, toks), toks)
        ysend[p] = acc[:, other, p * half : (p + 1) * half].astype(BF)
        return remote(ysend.at[p], yrecv.at[p], y_ssem.at[p], y_rsem.at[p], across)

    def projection_end(p, copy):
        copy.wait_recv()
        own = pl.ds(pl.multiple_of(y * toks, toks), toks)
        value = acc[:, own, p * half : (p + 1) * half] + yrecv[p].astype(F32)
        for col in range(CB):
            lo = col * bs + p * half
            pout[:, lo : lo + half] = value[col].astype(BF)

    make_weights(0)
    send_own(0)
    make_weights(1)
    acc[...] = jnp.zeros_like(acc)
    some(2)
    y_copy = {}
    steps = 2 * zs - 2
    for p in range(2):
        if p == 1:
            add_products(1, [(core, z)])
        else:
            add_products(0, [(core, z)])
        sib_step = 1
        pending = [(0, z)]
        for d in range(1, far + 1):
            arrived = []
            for k in range(2):
                for way in range(2):
                    order = k if way == 0 else 1 - k
                    if d <= reach(way, order):
                        ag[way, d, p, order].wait_recv()
                        if d < reach(way, order):
                            send_ring(way, behind(way, d), d + 1, p, order)
            if d < far:
                arrived = [behind(0, d), behind(1, d)]
            else:
                arrived = [behind(0, d)]
            fresh = []
            for zz in arrived:
                send_sibling(zz, sib_step, p)
                fresh.append((sib_step, zz))
                sib_step += 1
            if p == 0 and d == far - 1:
                send_own(1)
            some(2 if p == 0 else 3)
            items = [(core, zz) for zz in arrived]
            for step, zz in pending:
                sib[step, p].wait_recv()
                items.append((1 - core, zz))
            add_products(p, items)
            pending = fresh
        items = []
        for step, zz in pending:
            sib[step, p].wait_recv()
            items.append((1 - core, zz))
        add_products(p, items)
        y_copy[p] = projection_part(p)
    some(len(work))
    for p in range(2):
        projection_end(p, y_copy[p])
    stores.append(local(pout, proj_out, store_sem.at[6]))

    for copy in outgoing + own_to_sibling + forwarded:
        copy.wait_send()
    for group in (far_copy, near_copy, ag, sib, y_copy):
        for copy in group.values():
            copy.wait_send()
    for copy in stores:
        copy.wait()


def solution(mesh):
    zs = mesh.shape["dp"] // 4

    def on_device(act, og, table, plan, ls, rs, lr, rr, wb):
        toks = act.shape[0]
        bs = ls.shape[-1]
        rb = act.shape[1] // bs
        slots = table.shape[1]
        half = bs // 2
        mats = [value.reshape(bs, bs) for value in (ls, rs, lr, rr, wb)]
        far = zs // 2
        square = jax.ShapeDtypeStruct((bs, bs), F32)
        any_space = pl.BlockSpec(memory_space=pl.ANY)
        smem = pl.BlockSpec(memory_space=pltpu.SMEM)
        f_mat = pltpu.VMEM((bs, bs), F32)
        b_mat = pltpu.VMEM((bs, bs), BF)
        dma = pltpu.SemaphoreType.DMA
        outs = pl.pallas_call(
            functools.partial(kernel, zs, toks, rb, bs, slots),
            out_shape=[
                square,
                square,
                square,
                square,
                jax.ShapeDtypeStruct((bs, bs), BF),
                jax.ShapeDtypeStruct((toks, CB * bs), BF),
            ],
            in_specs=[smem, smem] + [any_space] * 7,
            out_specs=[any_space] * 6,
            scratch_shapes=[
                pltpu.VMEM((rb, 4 * toks, half), BF),
                pltpu.VMEM((rb, 4 * toks, half), BF),
                pltpu.VMEM((CB, 4 * toks, bs), BF),
                pltpu.VMEM((2, 2, half, half), BF),
                pltpu.VMEM((2, 2, half, half), BF),
                pltpu.VMEM((2, far - 1, 2, half, bs), BF),
                pltpu.VMEM((2, far - 1, 2, half, bs), BF),
                pltpu.VMEM((2, zs, 2, bs, half), BF),
                pltpu.VMEM((CB, 2 * toks, bs), F32),
                pltpu.VMEM((2, CB, toks, half), BF),
                pltpu.VMEM((2, CB, toks, half), BF),
                pltpu.VMEM((toks, CB * bs), BF),
                f_mat, f_mat, f_mat, f_mat, b_mat,
                b_mat, b_mat, b_mat, b_mat, b_mat, b_mat, b_mat, b_mat,
                f_mat, f_mat, f_mat, b_mat, b_mat, b_mat, b_mat, b_mat,
                dma((CB + 2 * rb + 5,)),
                dma((12,)), dma((12,)),
                dma((2, far, 2)), dma((2, far, 2)),
                dma((2, far, 2, 2)), dma((2, far, 2, 2)),
                dma((zs, 2)), dma((zs, 2)),
                dma((2,)), dma((2,)),
                dma((7,)),
            ],
            compiler_params=pltpu.CompilerParams(
                collective_id=0, has_side_effects=True, vmem_limit_bytes=56 * 1024 * 1024
            ),
        )(table, plan, act, og, *mats)
        return tuple(value.reshape(1, 1, bs, bs) for value in outs[:5]) + (outs[5],)

    block = P("mp", "dp", None, None)
    return jax.shard_map(
        on_device,
        mesh=mesh,
        in_specs=(P("dp", None), P("dp", "mp"), P(), P(), block, block, block, block, block),
        out_specs=(block, block, block, block, block, P("dp", "mp")),
        check_vma=False,
    )
```

```python
import functools

import jax
import jax.numpy as jnp
from jax import lax
from jax.experimental import pallas as pl
from jax.experimental.pallas import tpu as pltpu
from jax.sharding import PartitionSpec as P

BETA = 0.9
STEP = 0.1
EPS = 1e-06
CB = 4

STAGGER = False
LAG = 1

MESH = pl.DeviceIdType.MESH
BF = jnp.bfloat16
F32 = jnp.float32


def dot(left, right):
    return jnp.dot(left, right, preferred_element_type=F32)


def dot_tn(left, right):
    return lax.dot_general(left, right, (((0,), (0,)), ((), ())), preferred_element_type=F32)


def dot_nt(left, right):
    return lax.dot_general(left, right, (((1,), (1,)), ((), ())), preferred_element_type=F32)


def split(value):
    high = value.astype(BF)
    return high, (value - high.astype(F32)).astype(BF)


def kernel(
    zs, toks, rb, bs, slots,
    table, plan, act, og, ls, rs, lr, rr, wb,
    nl, nr, lold, rold, nw, pout,
    a_lo, a_hi, e_lo, e_hi, far_s, far_r, near_s, near_r, wag, acc, ysend, yrecv,
    wold, lh, ll, rh, rl, gh, gl, th, tl, tf,
    nf, m1f, xf, mb0, mb1, nb, kb, xb,
    gate, load_sem, p0_send, p0_recv, rs_send, rs_recv, ag_send, ag_recv, sib_send, sib_recv, y_ssem, y_rsem,
):
    half = bs // 2
    quarter = bs // 4
    far = zs // 2
    nblk = rb * CB
    dp = lax.axis_index("dp")
    mp = lax.axis_index("mp")
    core = lax.rem(dp, 2)
    z = lax.rem(dp // 2, zs)
    y = dp // (2 * zs)

    def device(yy, zz, cc):
        return yy * (2 * zs) + zz * 2 + cc

    up = lax.rem(z + 1, zs)
    down = lax.rem(z + zs - 1, zs)
    ring = ((device(y, up, core), mp), (device(y, down, core), mp))
    sibling = (device(y, z, 1 - core), mp)
    across = (device(1 - y, z, core), mp)
    across_other = (device(1 - y, z, core), mp + 1 - 2 * lax.rem(mp, 2))

    def remote(src, dst, send, recv, to):
        copy = pltpu.make_async_remote_copy(
            src_ref=src, dst_ref=dst, send_sem=send, recv_sem=recv, device_id=to, device_id_type=MESH
        )
        copy.start()
        return copy

    def rows_of(yy, cc):
        return pl.ds(pl.multiple_of((cc * 2 + yy) * toks, toks), toks)

    def local(src, dst, sem):
        copy = pltpu.make_async_copy(src, dst, sem)
        copy.start()
        return copy

    mine = rows_of(y, core)
    loads = {}
    for h, (e_dst, a_dst) in enumerate(((e_lo, a_lo), (e_hi, a_hi))):
        first = h * (CB + rb)
        loads["e", h] = [
            local(og.at[:, k * bs + h * half : k * bs + (h + 1) * half], e_dst.at[k, mine, :], load_sem.at[first + k])
            for k in range(CB)
        ]
        loads["a", h] = [
            local(act.at[:, r * bs + h * half : r * bs + (h + 1) * half], a_dst.at[r, mine, :], load_sem.at[first + CB + r])
            for r in range(rb)
        ]
    base = 2 * (CB + rb)
    load_mats = [
        local(src, dst, load_sem.at[base + k])
        for k, (src, dst) in enumerate(((lr, lold), (rr, rold), (wb, wold), (ls, nl), (rs, nr)))
    ]

    barrier = pltpu.get_barrier_semaphore()
    for other in (sibling, across, across_other) + ring:
        pl.semaphore_signal(barrier, inc=1, device_id=other, device_id_type=MESH)
    pl.semaphore_wait(barrier, 5)

    def part(number, rows):
        return (
            e_lo.at[:, rows, :],
            a_lo.at[rb - 2 : rb, rows, :],
            a_lo.at[0 : rb - 2, rows, :],
            e_hi.at[:, rows, :],
            a_hi.at[rb - 1 : rb, rows, :],
            a_hi.at[0 : rb - 1, rows, :],
        )[number]

    parts = 6

    def send_part(number, rows, slot, to):
        ref = part(number, rows)
        return remote(ref, ref, p0_send.at[slot], p0_recv.at[slot], to)

    outgoing = {}
    to_sibling = {}
    forwarded = {}
    for what, numbers in ((("e", 0), (0,)), (("a", 0), (1, 2)), (("e", 1), (3,)), (("a", 1), (4, 5))):
        for copy in loads[what]:
            copy.wait()
        if numbers == (3,):
            for number in (0, 1, 2):
                outgoing[number].wait_send()
        for number in numbers:
            to = across_other if number in (2, 5) else across
            outgoing[number] = send_part(number, mine, number, to)
            to_sibling[number] = send_part(number, mine, parts + number, sibling)
    theirs = rows_of(1 - y, core)

    def forward(numbers):
        for number in numbers:
            outgoing[number].wait_recv()
            forwarded[number] = send_part(number, theirs, 2 * parts + number, sibling)

    def have(numbers):
        for number in numbers:
            to_sibling[number].wait_recv()
            forwarded[number].wait_recv()

    def block_at(zz, cc):
        return table[mp, y * (2 * zs) + zz * 2 + cc]

    def row_and_col(block):
        safe = jnp.where(block < nblk, block, 0)
        return safe // CB, lax.rem(safe, CB)

    def partial_grad(zz, i, j):
        r, c = row_and_col(block_at(zz, core))
        return dot_tn((a_lo, a_hi)[i][r], (e_lo, e_hi)[j][c])

    far_copy = {}
    near_copy = {}

    def send_far(i, j):
        value = partial_grad(lax.rem(z + far, zs), i, j).astype(BF)
        for way in range(2):
            far_s[way, i, j] = value[way * quarter : (way + 1) * quarter, :]
            far_copy[way, i, j] = remote(
                far_s.at[way, i, j], far_r.at[way, i, j], rs_send.at[way, 0, i, j], rs_recv.at[way, 0, i, j], ring[way]
            )

    def send_near(d, i, j):
        for way in range(2):
            zz = lax.rem(z + d, zs) if way == 0 else lax.rem(z + zs - d, zs)
            value = partial_grad(zz, i, j)
            if d == far - 1:
                rows = slice(way * quarter, (way + 1) * quarter)
                rest = slice((1 - way) * quarter, (2 - way) * quarter)
                near_s[way, d - 1, i, j, rest, :] = value[rest, :].astype(BF)
                far_copy[way, i, j].wait_recv()
                near_s[way, d - 1, i, j, rows, :] = (value[rows, :] + far_r[way, i, j].astype(F32)).astype(BF)
            else:
                near_copy[way, d + 1, i, j].wait_recv()
                near_s[way, d - 1, i, j] = (value + near_r[way, d, i, j].astype(F32)).astype(BF)
            near_copy[way, d, i, j] = remote(
                near_s.at[way, d - 1, i, j],
                near_r.at[way, d - 1, i, j],
                rs_send.at[way, d, i, j],
                rs_recv.at[way, d, i, j],
                ring[way],
            )

    forward((0, 1, 2))
    have((0, 1, 2))
    if STAGGER:

        @pl.when(core == 1)
        def _():
            pl.semaphore_wait(gate, 1)

    send_far(0, 0)
    send_near(far - 1, 0, 0)
    if STAGGER:

        @pl.when(core == 0)
        def _():
            pl.semaphore_signal(gate, inc=1, device_id=sibling, device_id_type=MESH)

    forward((3,))
    have((3,))
    send_far(0, 1)
    send_near(far - 1, 0, 1)
    forward((4, 5))
    have((4, 5))
    send_far(1, 0)
    send_far(1, 1)
    for copy in load_mats:
        copy.wait()
    lh[...], ll[...] = split(lold[...])
    rh[...], rl[...] = split(rold[...])
    quarters = ((0, 0), (0, 1), (1, 0), (1, 1))
    order = sorted((2 * (far - 1 - d) + (0, 0.6, 1.1, 1.6)[n], d, q) for d in range(far - 1, 0, -1) for n, q in enumerate(quarters))
    for _, d, (i, j) in order:
        if (d, i, j) not in ((far - 1, 0, 0), (far - 1, 0, 1)):
            send_near(d, i, j)
    own_block = block_at(z, core)
    filled = jnp.where(own_block < nblk, 1.0, 0.0).astype(F32)
    lefts = [None, None]
    for i, j in quarters:
        rows = slice(i * half, (i + 1) * half)
        cols = slice(j * half, (j + 1) * half)
        value = partial_grad(z, i, j)
        near_copy[0, 1, i, j].wait_recv()
        near_copy[1, 1, i, j].wait_recv()
        value = (value + near_r[0, 0, i, j].astype(F32) + near_r[1, 0, i, j].astype(F32)) * filled
        high, low = split(value)
        gh[rows, cols] = high
        gl[rows, cols] = low
        term = dot(lh[:, rows], high) + dot(lh[:, rows], low) + dot(ll[:, rows], high)
        lefts[j] = term if i == 0 else lefts[j] + term
        if i == 1:
            th[:, cols], tl[:, cols] = split(lefts[j])
            if j == 0:
                tf[...] = dot(th[:, cols], rh[cols, 0:half]) + dot(th[:, cols], rl[cols, 0:half]) + dot(tl[:, cols], rh[cols, 0:half])

    ag = {}
    sib = {}

    def piece(cc, zz, p, k):
        return wag.at[cc, zz, p, :, k * quarter : (k + 1) * quarter]

    def send_ring(way, zz, d, p, k):
        ref = piece(core, zz, p, k)
        ag[way, d, p, k] = remote(ref, ref, ag_send.at[way, d - 1, p, k], ag_recv.at[way, d - 1, p, k], ring[way])

    def send_sibling(zz, step, p):
        ref = wag.at[core, zz, p]
        sib[step, p] = remote(ref, ref, sib_send.at[step, p], sib_recv.at[step, p], sibling)

    def reach(way, k):
        return far if way == k else far - 1

    def behind(way, d):
        return lax.rem(z + zs - d, zs) if way == 0 else lax.rem(z + d, zs)

    def make_weights(p):
        cols = slice(p * half, (p + 1) * half)
        if p == 0:
            rows = slice(half, bs)
            update = tf[...]
        else:
            rows = slice(0, bs)
            update = 0.0
        update += dot(th[:, rows], rh[rows, cols]) + dot(th[:, rows], rl[rows, cols]) + dot(tl[:, rows], rh[rows, cols])
        value = (wold[:, cols].astype(F32) - STEP * update).astype(BF)
        wag[core, z, p] = value
        nw[:, cols] = value

    def send_own(p):
        for k in range(2):
            for way in range(2):
                order = k if way == 0 else 1 - k
                send_ring(way, z, 1, p, order)
        send_sibling(z, 0, p)

    def add_products(p, items):
        lo, hi = p * half, (p + 1) * half
        terms = []
        for cc, zz in items:
            block = block_at(zz, cc)
            r, c = row_and_col(block)
            rows = pl.ds(pl.multiple_of(core * (2 * toks), 2 * toks), 2 * toks)
            term = dot(a_lo[r, rows, :], wag[cc, zz, p, 0:half, :]) + dot(a_hi[r, rows, :], wag[cc, zz, p, half:bs, :])
            terms.append((block, c, term))
        for col in range(CB):
            value = acc[col, :, lo:hi]
            for block, c, term in terms:
                weight = jnp.where((block < nblk) & (c == col), 1.0, 0.0).astype(F32)
                value = value + term * weight
            acc[col, :, lo:hi] = value

    own_flag = jnp.zeros((), jnp.int32)
    for k in range(plan.shape[1]):
        own_flag = jnp.where(plan[mp, k] == own_block, 1, own_flag)
    own_flag = jnp.where(own_block < nblk, own_flag, 0)

    def new_left():
        nl[...] = BETA * nl[...] + dot_nt(gh[...], gh[...]) + dot_nt(gh[...], gl[...]) + dot_nt(gl[...], gh[...])

    def new_right():
        nr[...] = BETA * nr[...] + dot_tn(gh[...], gh[...]) + dot_tn(gh[...], gl[...]) + dot_tn(gl[...], gh[...])

    width = half

    def eye_tile(lo):
        rows = lax.broadcasted_iota(jnp.int32, (bs, width), 0)
        cols = lax.broadcasted_iota(jnp.int32, (bs, width), 1) + lo
        return jnp.where(rows == cols, 1.0, 0.0).astype(F32)

    def tiles(body):
        for lo in range(0, bs, width):
            body(slice(lo, lo + width), lo)

    def newton(stats, old):
        scale = {}

        def start():
            total = jnp.sum(stats[...] * stats[...], axis=(0, 1), keepdims=True)
            scale["z"] = 5.0 / (2.0 * jnp.sqrt(total + EPS))
            scale["root"] = jnp.sqrt(jnp.sqrt(scale["z"]))
            mb0[...] = (scale["z"] * stats[...]).astype(BF)

            def body(cols, lo):
                value = (-0.625 * scale["z"]) * stats[:, cols] + 0.0625 * dot(mb0[...], mb0[:, cols])
                nf[:, cols] = value
                nb[:, cols] = value.astype(BF)

            tiles(body)

        def fourth_power():
            def body(cols, lo):
                kb[:, cols] = (3.125 * nf[:, cols] + dot(nb[...], nb[:, cols])).astype(BF)

            tiles(body)

        def first_coupled():
            def body(cols, lo):
                value = (2.44140625 * scale["z"]) * stats[:, cols] + dot(kb[...], mb0[:, cols])
                m1f[:, cols] = value
                mb1[:, cols] = value.astype(BF)

            tiles(body)

        def second_iterate():
            def body(cols, lo):
                value = 1.5625 * eye_tile(lo) - 0.3125 * (scale["z"] * stats[:, cols] + m1f[:, cols])
                value = scale["root"] * (value + 0.0625 * dot(mb0[...], mb1[:, cols]))
                xf[:, cols] = value
                xb[:, cols] = value.astype(BF)

            tiles(body)

        def second_square():
            def body(cols, lo):
                value = -0.625 * m1f[:, cols] + 0.0625 * dot(mb1[...], mb1[:, cols])
                nf[:, cols] = value
                nb[:, cols] = value.astype(BF)

            tiles(body)

        def second_coupled():
            def body(cols, lo):
                mb0[:, cols] = (2.44140625 * m1f[:, cols] + dot(kb[...], mb1[:, cols])).astype(BF)

            tiles(body)

        def finish():
            mask = jnp.full((bs, width), own_flag, jnp.int32) > 0

            def body(cols, lo):
                value = 1.25 * xf[:, cols] - 0.25 * dot(xb[...], mb0[:, cols])
                old[:, cols] = jnp.where(mask, value, old[:, cols])

            tiles(body)

        return [start, fourth_power, first_coupled, second_iterate, second_square, fourth_power, second_coupled, finish]

    work = [new_left, new_right] + newton(nl, lold) + newton(nr, rold)

    def some(count):
        for _ in range(count):
            if work:
                work.pop(0)()

    def projection_part(p):
        other = pl.ds(pl.multiple_of((1 - y) * toks, toks), toks)
        ysend[p] = acc[:, other, p * half : (p + 1) * half].astype(BF)
        return remote(ysend.at[p], yrecv.at[p], y_ssem.at[p], y_rsem.at[p], across)

    def projection_end(p, copy):
        copy.wait_recv()
        own = pl.ds(pl.multiple_of(y * toks, toks), toks)
        value = acc[:, own, p * half : (p + 1) * half] + yrecv[p].astype(F32)
        for col in range(CB):
            lo = col * bs + p * half
            pout[:, lo : lo + half] = value[col].astype(BF)

    make_weights(0)
    send_own(0)
    make_weights(1)
    acc[...] = jnp.zeros_like(acc)
    some(2)
    y_copy = {}
    for p in range(2):
        if p == 1:
            add_products(1, [(core, z)])
        else:
            add_products(0, [(core, z)])
        sib_step = 1
        pending = [[(0, z)]]
        for d in range(1, far + 1):
            for k in range(2):
                for way in range(2):
                    order = k if way == 0 else 1 - k
                    if d <= reach(way, order):
                        ag[way, d, p, order].wait_recv()
                        if d < reach(way, order):
                            send_ring(way, behind(way, d), d + 1, p, order)
            arrived = [behind(0, d), behind(1, d)] if d < far else [behind(0, d)]
            fresh = []
            for zz in arrived:
                send_sibling(zz, sib_step, p)
                fresh.append((sib_step, zz))
                sib_step += 1
            pending.append(fresh)
            if p == 0 and d == far - 1:
                send_own(1)
            some(2 if p == 0 else 3)
            items = [(core, zz) for zz in arrived]
            if len(pending) > LAG:
                for step, zz in pending.pop(0):
                    sib[step, p].wait_recv()
                    items.append((1 - core, zz))
            add_products(p, items)
        items = []
        for step, zz in sum(pending, []):
            sib[step, p].wait_recv()
            items.append((1 - core, zz))
        add_products(p, items)
        y_copy[p] = projection_part(p)
    some(len(work))
    for p in range(2):
        projection_end(p, y_copy[p])

    for number in (3, 4, 5):
        outgoing[number].wait_send()
    for group in (to_sibling, forwarded, far_copy, near_copy, ag, sib, y_copy):
        for copy in group.values():
            copy.wait_send()


def hand_over(*refs):
    count = (len(refs) - 1) // 2
    sems = refs[-1]
    copies = [pltpu.make_async_copy(refs[k], refs[count + k], sems.at[k]) for k in range(count)]
    for copy in copies:
        copy.start()
    for copy in copies:
        copy.wait()


def solution(mesh):
    zs = mesh.shape["dp"] // 4

    def on_device(act, og, table, plan, ls, rs, lr, rr, wb):
        toks = act.shape[0]
        bs = ls.shape[-1]
        rb = act.shape[1] // bs
        slots = table.shape[1]
        half = bs // 2
        quarter = bs // 4
        mats = [value.reshape(bs, bs) for value in (ls, rs, lr, rr, wb)]
        far = zs // 2
        leaves = [jax.ShapeDtypeStruct((bs, bs), F32)] * 4
        leaves += [jax.ShapeDtypeStruct((bs, bs), BF), jax.ShapeDtypeStruct((toks, CB * bs), BF)]
        vmem = pl.BlockSpec(memory_space=pltpu.VMEM)
        any_space = pl.BlockSpec(memory_space=pl.ANY)
        smem = pl.BlockSpec(memory_space=pltpu.SMEM)
        f_mat = pltpu.VMEM((bs, bs), F32)
        b_mat = pltpu.VMEM((bs, bs), BF)
        dma = pltpu.SemaphoreType.DMA
        outs = pl.pallas_call(
            functools.partial(kernel, zs, toks, rb, bs, slots),
            out_shape=[pltpu.VMEM(leaf.shape, leaf.dtype) for leaf in leaves],
            in_specs=[smem, smem] + [any_space] * 7,
            out_specs=[vmem] * 6,
            scratch_shapes=[
                pltpu.VMEM((rb, 4 * toks, half), BF),
                pltpu.VMEM((rb, 4 * toks, half), BF),
                pltpu.VMEM((CB, 4 * toks, half), BF),
                pltpu.VMEM((CB, 4 * toks, half), BF),
                pltpu.VMEM((2, 2, 2, quarter, half), BF),
                pltpu.VMEM((2, 2, 2, quarter, half), BF),
                pltpu.VMEM((2, far - 1, 2, 2, half, half), BF),
                pltpu.VMEM((2, far - 1, 2, 2, half, half), BF),
                pltpu.VMEM((2, zs, 2, bs, half), BF),
                pltpu.VMEM((CB, 2 * toks, bs), F32),
                pltpu.VMEM((2, CB, toks, half), BF),
                pltpu.VMEM((2, CB, toks, half), BF),
                b_mat,
                b_mat, b_mat, b_mat, b_mat, b_mat, b_mat, b_mat, b_mat,
                pltpu.VMEM((bs, half), F32),
                f_mat, f_mat, f_mat, b_mat, b_mat, b_mat, b_mat, b_mat,
                pltpu.SemaphoreType.REGULAR,
                dma((2 * (CB + rb) + 5,)),
                dma((18,)), dma((18,)),
                dma((2, far, 2, 2)), dma((2, far, 2, 2)),
                dma((2, far, 2, 2)), dma((2, far, 2, 2)),
                dma((zs, 2)), dma((zs, 2)),
                dma((2,)), dma((2,)),
            ],
            compiler_params=pltpu.CompilerParams(
                collective_id=0, has_side_effects=True, vmem_limit_bytes=57 * 1024 * 1024
            ),
        )(table, plan, act, og, *mats)
        outs = pl.pallas_call(
            hand_over,
            out_shape=leaves,
            in_specs=[vmem] * 6,
            out_specs=[any_space] * 6,
            scratch_shapes=[dma((6,))],
            compiler_params=pltpu.CompilerParams(vmem_limit_bytes=4 * 1024 * 1024),
        )(*[pltpu.with_memory_space_constraint(value, pltpu.VMEM) for value in outs])
        return tuple(value.reshape(1, 1, bs, bs) for value in outs[:5]) + (outs[5],)

    block = P("mp", "dp", None, None)
    return jax.shard_map(
        on_device,
        mesh=mesh,
        in_specs=(P("dp", None), P("dp", "mp"), P(), P(), block, block, block, block, block),
        out_specs=(block, block, block, block, block, P("dp", "mp")),
        check_vma=False,
    )
```

```python
import functools

import jax
import jax.numpy as jnp
from jax import lax
from jax.experimental import pallas as pl
from jax.experimental.pallas import tpu as pltpu
from jax.sharding import PartitionSpec as P

BETA = 0.9
STEP = 0.1
EPS = 1e-06
CB = 4

PACE = 3

MESH = pl.DeviceIdType.MESH
BF = jnp.bfloat16
F32 = jnp.float32


def dot(left, right):
    return jnp.dot(left, right, preferred_element_type=F32)


def dot_tn(left, right):
    return lax.dot_general(left, right, (((0,), (0,)), ((), ())), preferred_element_type=F32)


def dot_nt(left, right):
    return lax.dot_general(left, right, (((1,), (1,)), ((), ())), preferred_element_type=F32)


def split(value):
    high = value.astype(BF)
    return high, (value - high.astype(F32)).astype(BF)


def kernel(
    zs, toks, rb, bs, slots,
    table, plan, act, og, ls, rs, lr, rr, wb,
    nl, nr, lold, rold, nw, pout,
    a_0, a_1, a_2, e_0, e_1, far_s, far_r, near_s, near_r, wag_0, wag_1, acc, ysend_0, ysend_1, yrecv_0, yrecv_1,
    wold, mid, lh, ll, rh, rl, gh, gl, th, tl, tf,
    nf, m1f, xf, mb0, mb1, nb, kb, xb,
    load_sem, p0_send, p0_recv, rs_send, rs_recv, ag_send, ag_recv, sib_send, sib_recv, y_ssem, y_rsem,
):
    half = bs // 2
    quarter = bs // 4
    far = zs // 2
    a_parts, e_parts = (a_0, a_1, a_2), (e_0, e_1)
    a_cols = ((0, quarter), (quarter, half), (half, bs))
    wags, ysends, yrecvs = (wag_0, wag_1), (ysend_0, ysend_1), (yrecv_0, yrecv_1)
    chunks = ((0, half), (half, bs))
    nblk = rb * CB
    dp = lax.axis_index("dp")
    mp = lax.axis_index("mp")
    core = lax.rem(dp, 2)
    z = lax.rem(dp // 2, zs)
    y = dp // (2 * zs)

    def device(yy, zz, cc):
        return yy * (2 * zs) + zz * 2 + cc

    up = lax.rem(z + 1, zs)
    down = lax.rem(z + zs - 1, zs)
    ring = ((device(y, up, core), mp), (device(y, down, core), mp))
    sibling = (device(y, z, 1 - core), mp)
    across = (device(1 - y, z, core), mp)
    across_other = (device(1 - y, z, core), mp + 1 - 2 * lax.rem(mp, 2))

    def remote(src, dst, send, recv, to):
        copy = pltpu.make_async_remote_copy(
            src_ref=src, dst_ref=dst, send_sem=send, recv_sem=recv, device_id=to, device_id_type=MESH
        )
        copy.start()
        return copy

    def rows_of(yy, cc):
        return pl.ds(pl.multiple_of((cc * 2 + yy) * toks, toks), toks)

    def local(src, dst, sem):
        copy = pltpu.make_async_copy(src, dst, sem)
        copy.start()
        return copy

    mine = rows_of(y, core)
    loads = {}
    base = 0
    for kind, i in (("e", 0), ("a", 0), ("a", 1), ("e", 1), ("a", 2)):
        source, dst, count = (og, e_parts[i], CB) if kind == "e" else (act, a_parts[i], rb)
        lo, hi = (i * half, (i + 1) * half) if kind == "e" else a_cols[i]
        loads[kind, i] = [
            local(source.at[:, k * bs + lo : k * bs + hi], dst.at[k, mine, :], load_sem.at[base + k]) for k in range(count)
        ]
        base += count
    load_mats = [
        local(src, dst, load_sem.at[base + k])
        for k, (src, dst) in enumerate(((lr, lold), (rr, rold), (wb, wold), (ls, nl), (rs, nr)))
    ]

    barrier = pltpu.get_barrier_semaphore()
    for other in (sibling, across, across_other) + ring:
        pl.semaphore_signal(barrier, inc=1, device_id=other, device_id_type=MESH)
    pl.semaphore_wait(barrier, 5)

    def part(number, rows):
        return (
            e_0.at[:, rows, :],
            a_0.at[:, rows, :],
            e_1.at[:, rows, :],
            a_1.at[:, rows, :],
            a_2.at[rb - 2 : rb, rows, :],
            a_2.at[0 : rb - 2, rows, :],
        )[number]

    parts = 6

    def send_part(number, rows, slot, to):
        ref = part(number, rows)
        return remote(ref, ref, p0_send.at[slot], p0_recv.at[slot], to)

    outgoing = {}
    to_sibling = {}
    forwarded = {}

    def send_parts(numbers, needs):
        for what in needs:
            for copy in loads[what]:
                copy.wait()
        for number in numbers:
            outgoing[number] = send_part(number, mine, number, across_other if number in (1, 3, 5) else across)
        for number in numbers:
            to_sibling[number] = send_part(number, mine, parts + number, sibling)

    def sent(numbers):
        for number in numbers:
            outgoing[number].wait_send()

    send_parts((0, 1), (("e", 0), ("a", 0)))
    sent((0, 1))
    send_parts((2, 3), (("e", 1), ("a", 1)))
    sent((2, 3))
    send_parts((4, 5), (("a", 2),))
    theirs = rows_of(1 - y, core)

    def forward(numbers):
        for number in numbers:
            outgoing[number].wait_recv()
            forwarded[number] = send_part(number, theirs, 2 * parts + number, sibling)

    def have(numbers):
        for number in numbers:
            to_sibling[number].wait_recv()
            forwarded[number].wait_recv()

    def block_at(zz, cc):
        return table[mp, y * (2 * zs) + zz * 2 + cc]

    def row_and_col(block):
        safe = jnp.where(block < nblk, block, 0)
        return safe // CB, lax.rem(safe, CB)

    def partial_grad(zz, piece):
        r, c = row_and_col(block_at(zz, core))
        return dot_tn(a_parts[piece[0]][r], e_parts[piece[1]][c])

    pieces = ((0, 0), (1, 0), (0, 1), (1, 1), (2, 0), (2, 1))
    rs_copy = {}

    def piece_rows(piece, part=None):
        lo, hi = a_cols[piece[0]]
        if part is None:
            return slice(lo, hi)
        middle = (lo + hi) // 2
        return slice(lo, middle) if part == 0 else slice(middle, hi)

    def send_sum(way, level, piece, src, dst):
        n = pieces.index(piece)
        rs_copy[way, level, piece] = remote(src, dst, rs_send.at[way, level, n], rs_recv.at[way, level, n], ring[way])

    def target(way, d):
        return lax.rem(z + d, zs) if way == 0 else lax.rem(z + zs - d, zs)

    def send_start(piece):
        j = piece[1]
        lo, hi = a_cols[piece[0]]
        middle = (hi - lo) // 2
        rows = slice(lo // 2, hi // 2)
        value = partial_grad(target(0, far), piece).astype(BF)
        for way in range(2):
            far_s[way, j, rows, :] = value[way * middle : (way + 1) * middle, :]
            send_sum(way, 0, piece, far_s.at[way, j, rows, :], far_r.at[way, j, rows, :])
        for way in range(2):
            rest = 1 - way
            value = partial_grad(target(way, far - 1), piece)
            rows = piece_rows(piece, rest)
            near_s[way, far - 2, j, rows, :] = value[rest * middle : (rest + 1) * middle, :].astype(BF)
            mid[way, j, lo // 2 : hi // 2, :] = value[way * middle : (way + 1) * middle, :]
            send_sum(way, far, piece, near_s.at[way, far - 2, j, rows, :], near_r.at[way, far - 2, j, rows, :])

    def send_near(d, piece):
        if d < 1:
            return
        j = piece[1]
        lo, hi = a_cols[piece[0]]
        for way in range(2):
            if d == far - 1:
                rows = piece_rows(piece, way)
                value = mid[way, j, lo // 2 : hi // 2, :]
                rs_copy[way, 0, piece].wait_recv()
                value = value + far_r[way, j, lo // 2 : hi // 2, :].astype(F32)
            else:
                rows = piece_rows(piece)
                value = partial_grad(target(way, d), piece)
                rs_copy[way, d + 1, piece].wait_recv()
                if d == far - 2:
                    rs_copy[way, far, piece].wait_recv()
                value = value + near_r[way, d, j, rows, :].astype(F32)
            near_s[way, d - 1, j, rows, :] = value.astype(BF)
            send_sum(way, d, piece, near_s.at[way, d - 1, j, rows, :], near_r.at[way, d - 1, j, rows, :])

    forward((0, 1))
    have((0, 1))
    send_start(pieces[0])
    forward((3,))
    have((3,))
    send_start(pieces[1])
    forward((2,))
    send_near(far - 1, pieces[0])
    have((2,))
    send_start(pieces[2])
    send_start(pieces[3])
    send_near(far - 1, pieces[1])
    send_near(far - 2, pieces[0])
    forward((4, 5))
    have((4, 5))
    send_start(pieces[4])
    send_start(pieces[5])
    send_near(far - 1, pieces[2])
    send_near(far - 1, pieces[3])
    send_near(far - 2, pieces[1])
    send_near(far - 1, pieces[4])
    send_near(far - 1, pieces[5])
    send_near(far - 2, pieces[2])
    send_near(far - 2, pieces[3])
    for copy in load_mats:
        copy.wait()
    lh[...], ll[...] = split(lold[...])
    rh[...], rl[...] = split(rold[...])
    send_near(far - 3, pieces[0])
    send_near(far - 3, pieces[1])
    send_near(far - 2, pieces[4])
    send_near(far - 2, pieces[5])
    for n in (2, 3, 4, 5):
        send_near(far - 3, pieces[n])
    own_block = block_at(z, core)
    filled = jnp.where(own_block < nblk, 1.0, 0.0).astype(F32)

    def sum_piece(piece):
        j = piece[1]
        rows = piece_rows(piece)
        cols = slice(j * half, (j + 1) * half)
        value = partial_grad(z, piece)
        for way in range(2):
            rs_copy[way, 1, piece].wait_recv()
            if far == 2:
                rs_copy[way, far, piece].wait_recv()
        value = (value + near_r[0, 0, j, rows, :].astype(F32) + near_r[1, 0, j, rows, :].astype(F32)) * filled
        gh[rows, cols], gl[rows, cols] = split(value)

    def left_term(i, j):
        rows, cols = slice(i * half, (i + 1) * half), slice(j * half, (j + 1) * half)
        return dot(lh[:, rows], gh[rows, cols]) + dot(lh[:, rows], gl[rows, cols]) + dot(ll[:, rows], gh[rows, cols])

    def right_term(j, lo, hi):
        rows = slice(j * half, (j + 1) * half)
        return dot(th[:, rows], rh[rows, lo:hi]) + dot(th[:, rows], rl[rows, lo:hi]) + dot(tl[:, rows], rh[rows, lo:hi])

    lefts = []
    for j in range(2):
        sum_piece((0, j))
        sum_piece((1, j))
        lefts.append(left_term(0, j))
    for j in range(2):
        sum_piece((2, j))
        cols = slice(j * half, (j + 1) * half)
        th[:, cols], tl[:, cols] = split(lefts[j] + left_term(1, j))
        if j == 0:
            tf[...] = right_term(0, *chunks[0])

    ag = {}
    sib = {}

    def piece(cc, zz, p, k):
        return wags[p].at[cc, zz, k * half : (k + 1) * half, :]

    def send_ring(way, zz, d, p, k):
        ref = piece(core, zz, p, k)
        ag[way, d, p, k] = remote(ref, ref, ag_send.at[way, d - 1, p, k], ag_recv.at[way, d - 1, p, k], ring[way])

    def send_sibling(zz, step, p):
        ref = wags[p].at[core, zz]
        sib[step, p] = remote(ref, ref, sib_send.at[step, p], sib_recv.at[step, p], sibling)

    def reach(way, k):
        return far if way == k else far - 1

    def behind(way, d):
        return lax.rem(z + zs - d, zs) if way == 0 else lax.rem(z + d, zs)

    def make_weights(p):
        lo, hi = chunks[p]
        update = (tf[...] if p == 0 else right_term(0, lo, hi)) + right_term(1, lo, hi)
        value = (wold[:, lo:hi].astype(F32) - STEP * update).astype(BF)
        wags[p][core, z] = value
        nw[:, lo:hi] = value

    def send_own(p, k):
        for way in range(2):
            send_ring(way, z, 1, p, k if way == 0 else 1 - k)

    def add_products(p, items):
        lo, hi = chunks[p]
        terms = []
        for cc, zz in items:
            block = block_at(zz, cc)
            r, c = row_and_col(block)
            rows = pl.ds(pl.multiple_of(core * (2 * toks), 2 * toks), 2 * toks)
            lhs = jnp.concatenate([a_0[r, rows, :], a_1[r, rows, :]], axis=1)
            term = dot(lhs, wags[p][cc, zz, 0:half, :]) + dot(a_2[r, rows, :], wags[p][cc, zz, half:bs, :])
            terms.append((block, c, term))
        for col in range(CB):
            value = acc[col, :, lo:hi]
            for block, c, term in terms:
                weight = jnp.where((block < nblk) & (c == col), 1.0, 0.0).astype(F32)
                value = value + term * weight
            acc[col, :, lo:hi] = value

    own_flag = jnp.zeros((), jnp.int32)
    for k in range(plan.shape[1]):
        own_flag = jnp.where(plan[mp, k] == own_block, 1, own_flag)
    own_flag = jnp.where(own_block < nblk, own_flag, 0)

    def new_left():
        nl[...] = BETA * nl[...] + dot_nt(gh[...], gh[...]) + dot_nt(gh[...], gl[...]) + dot_nt(gl[...], gh[...])

    def new_right():
        nr[...] = BETA * nr[...] + dot_tn(gh[...], gh[...]) + dot_tn(gh[...], gl[...]) + dot_tn(gl[...], gh[...])

    width = half

    def eye_tile(lo):
        rows = lax.broadcasted_iota(jnp.int32, (bs, width), 0)
        cols = lax.broadcasted_iota(jnp.int32, (bs, width), 1) + lo
        return jnp.where(rows == cols, 1.0, 0.0).astype(F32)

    def tiles(body):
        for lo in range(0, bs, width):
            body(slice(lo, lo + width), lo)

    def newton(stats, old):
        scale = {}

        def start():
            total = jnp.sum(stats[...] * stats[...], axis=(0, 1), keepdims=True)
            scale["z"] = 5.0 / (2.0 * jnp.sqrt(total + EPS))
            scale["root"] = jnp.sqrt(jnp.sqrt(scale["z"]))
            mb0[...] = (scale["z"] * stats[...]).astype(BF)

            def body(cols, lo):
                value = (-0.625 * scale["z"]) * stats[:, cols] + 0.0625 * dot(mb0[...], mb0[:, cols])
                nf[:, cols] = value
                nb[:, cols] = value.astype(BF)

            tiles(body)

        def fourth_power():
            def body(cols, lo):
                kb[:, cols] = (3.125 * nf[:, cols] + dot(nb[...], nb[:, cols])).astype(BF)

            tiles(body)

        def first_coupled():
            def body(cols, lo):
                value = (2.44140625 * scale["z"]) * stats[:, cols] + dot(kb[...], mb0[:, cols])
                m1f[:, cols] = value
                mb1[:, cols] = value.astype(BF)

            tiles(body)

        def second_iterate():
            def body(cols, lo):
                value = 1.5625 * eye_tile(lo) - 0.3125 * (scale["z"] * stats[:, cols] + m1f[:, cols])
                value = scale["root"] * (value + 0.0625 * dot(mb0[...], mb1[:, cols]))
                xf[:, cols] = value
                xb[:, cols] = value.astype(BF)

            tiles(body)

        def second_square():
            def body(cols, lo):
                value = -0.625 * m1f[:, cols] + 0.0625 * dot(mb1[...], mb1[:, cols])
                nf[:, cols] = value
                nb[:, cols] = value.astype(BF)

            tiles(body)

        def second_coupled():
            def body(cols, lo):
                mb0[:, cols] = (2.44140625 * m1f[:, cols] + dot(kb[...], mb1[:, cols])).astype(BF)

            tiles(body)

        def finish():
            mask = jnp.full((bs, width), own_flag, jnp.int32) > 0

            def body(cols, lo):
                value = 1.25 * xf[:, cols] - 0.25 * dot(xb[...], mb0[:, cols])
                old[:, cols] = jnp.where(mask, value, old[:, cols])

            tiles(body)

        return [start, fourth_power, first_coupled, second_iterate, second_square, fourth_power, second_coupled, finish]

    work = [new_left, new_right] + newton(nl, lold) + newton(nr, rold)

    def some(count):
        for _ in range(count):
            if work:
                work.pop(0)()

    def projection_part(p):
        other = pl.ds(pl.multiple_of((1 - y) * toks, toks), toks)
        ysends[p][...] = acc[:, other, chunks[p][0] : chunks[p][1]].astype(BF)
        return remote(ysends[p], yrecvs[p], y_ssem.at[p], y_rsem.at[p], across)

    def projection_end(p, copy):
        copy.wait_recv()
        own = pl.ds(pl.multiple_of(y * toks, toks), toks)
        lo, hi = chunks[p]
        value = acc[:, own, lo:hi] + yrecvs[p][...].astype(F32)
        for col in range(CB):
            pout[:, col * bs + lo : col * bs + hi] = value[col].astype(BF)

    y_copy = {}
    sib_steps = [1, 1]
    ready = []
    later = []

    def compute(count):
        for _ in range(count):
            if ready:
                ready.pop(0)()
            else:
                some(1)
        ready.extend(later)
        later.clear()

    def sibling_products(p, items):
        for step, _ in items:
            sib[step, p].wait_recv()
        add_products(p, [(1 - core, zz) for _, zz in items])

    def finish_chunk(p):
        y_copy[p] = projection_part(p)

    def receive(p, d, k):
        for way in range(2):
            order = k if way == 0 else 1 - k
            if d <= reach(way, order):
                ag[way, d, p, order].wait_recv()
                if d < reach(way, order):
                    send_ring(way, behind(way, d), d + 1, p, order)
        if k == 1 or d == far:
            arrived = [behind(0, d), behind(1, d)] if d < far else [behind(0, d)]
            fresh = []
            for zz in arrived:
                send_sibling(zz, sib_steps[p], p)
                fresh.append((sib_steps[p], zz))
                sib_steps[p] += 1
            ready.append(functools.partial(add_products, p, [(core, zz) for zz in arrived]))
            later.append(functools.partial(sibling_products, p, fresh))
            if d == far:
                later.append(functools.partial(finish_chunk, p))

    make_weights(0)
    send_own(0, 0)
    send_own(0, 1)
    send_sibling(z, 0, 0)
    make_weights(1)
    send_own(1, 0)
    send_sibling(z, 0, 1)
    acc[...] = jnp.zeros_like(acc)
    ready.append(functools.partial(add_products, 0, [(core, z)]))
    later.append(functools.partial(sibling_products, 0, [(0, z)]))
    compute(2)
    for d in range(1, far + 1):
        for k in range(2 if d < far else 1):
            receive(0, d, k)
            if d == 1 and k == 1:
                send_own(1, 1)
            compute(PACE)
            if (d, k) == (max(far - 2, 1), 1):
                receive(1, 1, 0)
                ready.append(functools.partial(add_products, 1, [(core, z)]))
                later.append(functools.partial(sibling_products, 1, [(0, z)]))
                compute(PACE)
            if (d, k) == (far - 1, 1):
                receive(1, 1, 1)
                compute(PACE)
    for d in range(2, far + 1):
        for k in range(2 if d < far else 1):
            receive(1, d, k)
            compute(PACE if d < far else 1)
    while ready:
        ready.pop(0)()
    some(len(work))
    for p in range(2):
        projection_end(p, y_copy[p])

    sent((4, 5))
    for group in (to_sibling, forwarded, rs_copy, ag, sib, y_copy):
        for copy in group.values():
            copy.wait_send()


def hand_over(*refs):
    count = (len(refs) - 1) // 2
    sems = refs[-1]
    copies = [pltpu.make_async_copy(refs[k], refs[count + k], sems.at[k]) for k in range(count)]
    for copy in copies:
        copy.start()
    for copy in copies:
        copy.wait()


def solution(mesh):
    zs = mesh.shape["dp"] // 4

    def on_device(act, og, table, plan, ls, rs, lr, rr, wb):
        toks = act.shape[0]
        bs = ls.shape[-1]
        rb = act.shape[1] // bs
        slots = table.shape[1]
        half = bs // 2
        quarter = bs // 4
        mats = [value.reshape(bs, bs) for value in (ls, rs, lr, rr, wb)]
        far = zs // 2
        leaves = [jax.ShapeDtypeStruct((bs, bs), F32)] * 4
        leaves += [jax.ShapeDtypeStruct((bs, bs), BF), jax.ShapeDtypeStruct((toks, CB * bs), BF)]
        vmem = pl.BlockSpec(memory_space=pltpu.VMEM)
        any_space = pl.BlockSpec(memory_space=pl.ANY)
        smem = pl.BlockSpec(memory_space=pltpu.SMEM)
        f_mat = pltpu.VMEM((bs, bs), F32)
        b_mat = pltpu.VMEM((bs, bs), BF)
        dma = pltpu.SemaphoreType.DMA
        outs = pl.pallas_call(
            functools.partial(kernel, zs, toks, rb, bs, slots),
            out_shape=[pltpu.VMEM(leaf.shape, leaf.dtype) for leaf in leaves],
            in_specs=[smem, smem] + [any_space] * 7,
            out_specs=[vmem] * 6,
            scratch_shapes=[
                pltpu.VMEM((rb, 4 * toks, quarter), BF),
                pltpu.VMEM((rb, 4 * toks, quarter), BF),
                pltpu.VMEM((rb, 4 * toks, half), BF),
                pltpu.VMEM((CB, 4 * toks, half), BF),
                pltpu.VMEM((CB, 4 * toks, half), BF),
                pltpu.VMEM((2, 2, half, half), BF),
                pltpu.VMEM((2, 2, half, half), BF),
                pltpu.VMEM((2, far - 1, 2, bs, half), BF),
                pltpu.VMEM((2, far - 1, 2, bs, half), BF),
                pltpu.VMEM((2, zs, bs, half), BF),
                pltpu.VMEM((2, zs, bs, half), BF),
                pltpu.VMEM((CB, 2 * toks, bs), F32),
                pltpu.VMEM((CB, toks, half), BF),
                pltpu.VMEM((CB, toks, half), BF),
                pltpu.VMEM((CB, toks, half), BF),
                pltpu.VMEM((CB, toks, half), BF),
                b_mat,
                pltpu.VMEM((2, 2, half, half), F32),
                b_mat, b_mat, b_mat, b_mat, b_mat, b_mat, b_mat, b_mat,
                pltpu.VMEM((bs, half), F32),
                f_mat, f_mat, f_mat, b_mat, b_mat, b_mat, b_mat, b_mat,
                dma((2 * CB + 3 * rb + 5,)),
                dma((18,)), dma((18,)),
                dma((2, far + 1, 6)), dma((2, far + 1, 6)),
                dma((2, far, 2, 2)), dma((2, far, 2, 2)),
                dma((zs, 2)), dma((zs, 2)),
                dma((2,)), dma((2,)),
            ],
            compiler_params=pltpu.CompilerParams(
                collective_id=0, has_side_effects=True, vmem_limit_bytes=57 * 1024 * 1024
            ),
        )(table, plan, act, og, *mats)
        outs = pl.pallas_call(
            hand_over,
            out_shape=leaves,
            in_specs=[vmem] * 6,
            out_specs=[any_space] * 6,
            scratch_shapes=[dma((6,))],
            compiler_params=pltpu.CompilerParams(vmem_limit_bytes=4 * 1024 * 1024),
        )(*[pltpu.with_memory_space_constraint(value, pltpu.VMEM) for value in outs])
        return tuple(value.reshape(1, 1, bs, bs) for value in outs[:5]) + (outs[5],)

    block = P("mp", "dp", None, None)
    return jax.shard_map(
        on_device,
        mesh=mesh,
        in_specs=(P("dp", None), P("dp", "mp"), P(), P(), block, block, block, block, block),
        out_specs=(block, block, block, block, block, P("dp", "mp")),
        check_vma=False,
    )
```

```python
import functools

import jax
import jax.numpy as jnp
from jax import lax
from jax.experimental import pallas as pl
from jax.experimental.pallas import tpu as pltpu
from jax.sharding import PartitionSpec as P

BETA = 0.9
STEP = 0.1
EPS = 1e-06
CB = 4

PACE = 3
SIBLING_LAG = 4

MESH = pl.DeviceIdType.MESH
BF = jnp.bfloat16
F32 = jnp.float32


def dot(left, right):
    return jnp.dot(left, right, preferred_element_type=F32)


def dot_tn(left, right):
    return lax.dot_general(left, right, (((0,), (0,)), ((), ())), preferred_element_type=F32)


def dot_nt(left, right):
    return lax.dot_general(left, right, (((1,), (1,)), ((), ())), preferred_element_type=F32)


def split(value):
    high = value.astype(BF)
    return high, (value - high.astype(F32)).astype(BF)


def kernel(
    zs, toks, rb, bs, slots,
    table, plan, act, og, ls, rs, lr, rr, wb,
    nl, nr, lold, rold, nw, pout,
    a_0, a_1, a_2, e_0, e_1, far_s, far_r, near_s, near_r, wag_0, wag_1, acc, ysend_0, ysend_1, yrecv_0, yrecv_1,
    wold, mid, lh, ll, rh, rl, gh, gl, th, tl, tf,
    nf, m1f, xf, mb0, mb1, nb, kb, xb,
    gate, load_sem, p0_send, p0_recv, rs_send, rs_recv, ag_send, ag_recv, sib_send, sib_recv, y_ssem, y_rsem,
):
    half = bs // 2
    quarter = bs // 4
    far = zs // 2
    a_parts, e_parts = (a_0, a_1, a_2), (e_0, e_1)
    a_cols = ((0, quarter), (quarter, half), (half, bs))
    wags, ysends, yrecvs = (wag_0, wag_1), (ysend_0, ysend_1), (yrecv_0, yrecv_1)
    chunks = ((0, half), (half, bs))
    nblk = rb * CB
    dp = lax.axis_index("dp")
    mp = lax.axis_index("mp")
    core = lax.rem(dp, 2)
    z = lax.rem(dp // 2, zs)
    y = dp // (2 * zs)

    def device(yy, zz, cc):
        return yy * (2 * zs) + zz * 2 + cc

    up = lax.rem(z + 1, zs)
    down = lax.rem(z + zs - 1, zs)
    ring = ((device(y, up, core), mp), (device(y, down, core), mp))
    sibling = (device(y, z, 1 - core), mp)
    across = (device(1 - y, z, core), mp)
    across_other = (device(1 - y, z, core), mp + 1 - 2 * lax.rem(mp, 2))

    def remote(src, dst, send, recv, to):
        copy = pltpu.make_async_remote_copy(
            src_ref=src, dst_ref=dst, send_sem=send, recv_sem=recv, device_id=to, device_id_type=MESH
        )
        copy.start()
        return copy

    def rows_of(yy, cc):
        return pl.ds(pl.multiple_of((cc * 2 + yy) * toks, toks), toks)

    def local(src, dst, sem):
        copy = pltpu.make_async_copy(src, dst, sem)
        copy.start()
        return copy

    mine = rows_of(y, core)
    loads = {}
    base = 0
    for kind, i in (("e", 0), ("a", 0), ("a", 1), ("e", 1), ("a", 2)):
        source, dst, count = (og, e_parts[i], CB) if kind == "e" else (act, a_parts[i], rb)
        lo, hi = (i * half, (i + 1) * half) if kind == "e" else a_cols[i]
        loads[kind, i] = [
            local(source.at[:, k * bs + lo : k * bs + hi], dst.at[k, mine, :], load_sem.at[base + k]) for k in range(count)
        ]
        base += count
    load_mats = [
        local(src, dst, load_sem.at[base + k])
        for k, (src, dst) in enumerate(((lr, lold), (rr, rold), (wb, wold), (ls, nl), (rs, nr)))
    ]

    barrier = pltpu.get_barrier_semaphore()
    for other in (sibling, across, across_other) + ring:
        pl.semaphore_signal(barrier, inc=1, device_id=other, device_id_type=MESH)
    pl.semaphore_wait(barrier, 5)

    def part(number, rows):
        return (
            e_0.at[:, rows, :],
            a_0.at[:, rows, :],
            e_1.at[:, rows, :],
            a_1.at[:, rows, :],
            a_2.at[rb - 2 : rb, rows, :],
            a_2.at[0 : rb - 2, rows, :],
        )[number]

    parts = 6

    def send_part(number, rows, slot, to):
        ref = part(number, rows)
        return remote(ref, ref, p0_send.at[slot], p0_recv.at[slot], to)

    outgoing = {}
    to_sibling = {}
    forwarded = {}

    def send_parts(numbers, needs):
        for what in needs:
            for copy in loads[what]:
                copy.wait()
        for number in numbers:
            outgoing[number] = send_part(number, mine, number, across_other if number in (1, 3, 5) else across)
        for number in numbers:
            to_sibling[number] = send_part(number, mine, parts + number, sibling)

    def sent(numbers):
        for number in numbers:
            outgoing[number].wait_send()

    send_parts((0, 1), (("e", 0), ("a", 0)))
    sent((0, 1))
    send_parts((2, 3), (("e", 1), ("a", 1)))
    sent((2, 3))
    send_parts((4, 5), (("a", 2),))
    theirs = rows_of(1 - y, core)

    def forward(numbers):
        for number in numbers:
            outgoing[number].wait_recv()
            forwarded[number] = send_part(number, theirs, 2 * parts + number, sibling)

    def have(numbers):
        for number in numbers:
            to_sibling[number].wait_recv()
            forwarded[number].wait_recv()

    def block_at(zz, cc):
        return table[mp, y * (2 * zs) + zz * 2 + cc]

    def row_and_col(block):
        safe = jnp.where(block < nblk, block, 0)
        return safe // CB, lax.rem(safe, CB)

    def partial_grad(zz, piece):
        r, c = row_and_col(block_at(zz, core))
        return dot_tn(a_parts[piece[0]][r], e_parts[piece[1]][c])

    pieces = ((0, 0), (1, 0), (0, 1), (1, 1), (2, 0), (2, 1))
    rs_copy = {}

    def piece_rows(piece, part=None):
        lo, hi = a_cols[piece[0]]
        if part is None:
            return slice(lo, hi)
        middle = (lo + hi) // 2
        return slice(lo, middle) if part == 0 else slice(middle, hi)

    def send_sum(way, level, piece, src, dst):
        n = pieces.index(piece)
        rs_copy[way, level, piece] = remote(src, dst, rs_send.at[way, level, n], rs_recv.at[way, level, n], ring[way])

    def target(way, d):
        return lax.rem(z + d, zs) if way == 0 else lax.rem(z + zs - d, zs)

    def send_start(piece):
        j = piece[1]
        lo, hi = a_cols[piece[0]]
        middle = (hi - lo) // 2
        rows = slice(lo // 2, hi // 2)
        value = partial_grad(target(0, far), piece).astype(BF)
        for way in range(2):
            far_s[way, j, rows, :] = value[way * middle : (way + 1) * middle, :]
            send_sum(way, 0, piece, far_s.at[way, j, rows, :], far_r.at[way, j, rows, :])
        for way in range(2):
            rest = 1 - way
            value = partial_grad(target(way, far - 1), piece)
            rows = piece_rows(piece, rest)
            near_s[way, far - 2, j, rows, :] = value[rest * middle : (rest + 1) * middle, :].astype(BF)
            mid[way, j, lo // 2 : hi // 2, :] = value[way * middle : (way + 1) * middle, :]
            send_sum(way, far, piece, near_s.at[way, far - 2, j, rows, :], near_r.at[way, far - 2, j, rows, :])

    def send_near(d, piece):
        if d < 1:
            return
        j = piece[1]
        lo, hi = a_cols[piece[0]]
        for way in range(2):
            if d == far - 1:
                rows = piece_rows(piece, way)
                value = mid[way, j, lo // 2 : hi // 2, :]
                rs_copy[way, 0, piece].wait_recv()
                value = value + far_r[way, j, lo // 2 : hi // 2, :].astype(F32)
            else:
                rows = piece_rows(piece)
                value = partial_grad(target(way, d), piece)
                rs_copy[way, d + 1, piece].wait_recv()
                if d == far - 2:
                    rs_copy[way, far, piece].wait_recv()
                value = value + near_r[way, d, j, rows, :].astype(F32)
            near_s[way, d - 1, j, rows, :] = value.astype(BF)
            send_sum(way, d, piece, near_s.at[way, d - 1, j, rows, :], near_r.at[way, d - 1, j, rows, :])

    forward((0, 1))
    have((0, 1))
    send_start(pieces[0])
    forward((3,))
    have((3,))
    send_start(pieces[1])
    forward((2,))
    send_near(far - 1, pieces[0])
    have((2,))
    send_start(pieces[2])
    send_start(pieces[3])
    send_near(far - 1, pieces[1])
    send_near(far - 2, pieces[0])
    forward((4, 5))
    have((4, 5))
    send_start(pieces[4])
    send_start(pieces[5])
    send_near(far - 1, pieces[2])
    send_near(far - 1, pieces[3])
    send_near(far - 2, pieces[1])
    send_near(far - 1, pieces[4])
    send_near(far - 1, pieces[5])
    send_near(far - 2, pieces[2])
    send_near(far - 2, pieces[3])
    for copy in load_mats:
        copy.wait()
    lh[...], ll[...] = split(lold[...])
    rh[...], rl[...] = split(rold[...])
    send_near(far - 3, pieces[0])
    send_near(far - 3, pieces[1])

    @pl.when(core == 1)
    def _():
        pl.semaphore_wait(gate, 1)

    send_near(far - 2, pieces[4])
    send_near(far - 2, pieces[5])
    send_near(far - 3, pieces[2])
    send_near(far - 3, pieces[3])
    send_near(far - 3, pieces[4])
    send_near(far - 3, pieces[5])

    @pl.when(core == 0)
    def _():
        pl.semaphore_signal(gate, inc=1, device_id=sibling, device_id_type=MESH)

    own_block = block_at(z, core)
    filled = jnp.where(own_block < nblk, 1.0, 0.0).astype(F32)

    def sum_piece(piece):
        j = piece[1]
        rows = piece_rows(piece)
        cols = slice(j * half, (j + 1) * half)
        value = partial_grad(z, piece)
        for way in range(2):
            rs_copy[way, 1, piece].wait_recv()
            if far == 2:
                rs_copy[way, far, piece].wait_recv()
        value = (value + near_r[0, 0, j, rows, :].astype(F32) + near_r[1, 0, j, rows, :].astype(F32)) * filled
        gh[rows, cols], gl[rows, cols] = split(value)

    def left_term(i, j):
        rows, cols = slice(i * half, (i + 1) * half), slice(j * half, (j + 1) * half)
        return dot(lh[:, rows], gh[rows, cols]) + dot(lh[:, rows], gl[rows, cols]) + dot(ll[:, rows], gh[rows, cols])

    def right_term(j, lo, hi):
        rows = slice(j * half, (j + 1) * half)
        return dot(th[:, rows], rh[rows, lo:hi]) + dot(th[:, rows], rl[rows, lo:hi]) + dot(tl[:, rows], rh[rows, lo:hi])

    lefts = []
    for j in range(2):
        sum_piece((0, j))
        sum_piece((1, j))
        lefts.append(left_term(0, j))
    for j in range(2):
        sum_piece((2, j))
        cols = slice(j * half, (j + 1) * half)
        th[:, cols], tl[:, cols] = split(lefts[j] + left_term(1, j))
        if j == 0:
            tf[...] = right_term(0, *chunks[0])

    ag = {}
    sib = {}

    def piece(cc, zz, p, k):
        return wags[p].at[cc, zz, k * half : (k + 1) * half, :]

    def send_ring(way, zz, d, p, k):
        ref = piece(core, zz, p, k)
        ag[way, d, p, k] = remote(ref, ref, ag_send.at[way, d - 1, p, k], ag_recv.at[way, d - 1, p, k], ring[way])

    def send_sibling(zz, step, p):
        ref = wags[p].at[core, zz]
        sib[step, p] = remote(ref, ref, sib_send.at[step, p], sib_recv.at[step, p], sibling)

    def reach(way, k):
        return far if way == k else far - 1

    def behind(way, d):
        return lax.rem(z + zs - d, zs) if way == 0 else lax.rem(z + d, zs)

    def make_weights(p):
        lo, hi = chunks[p]
        update = (tf[...] if p == 0 else right_term(0, lo, hi)) + right_term(1, lo, hi)
        value = (wold[:, lo:hi].astype(F32) - STEP * update).astype(BF)
        wags[p][core, z] = value
        nw[:, lo:hi] = value

    def send_own(p, k):
        for way in range(2):
            send_ring(way, z, 1, p, k if way == 0 else 1 - k)

    def add_products(p, items):
        lo, hi = chunks[p]
        terms = []
        for cc, zz in items:
            block = block_at(zz, cc)
            r, c = row_and_col(block)
            rows = pl.ds(pl.multiple_of(core * (2 * toks), 2 * toks), 2 * toks)
            lhs = jnp.concatenate([a_0[r, rows, :], a_1[r, rows, :]], axis=1)
            term = dot(lhs, wags[p][cc, zz, 0:half, :]) + dot(a_2[r, rows, :], wags[p][cc, zz, half:bs, :])
            terms.append((block, c, term))
        for col in range(CB):
            value = acc[col, :, lo:hi]
            for block, c, term in terms:
                weight = jnp.where((block < nblk) & (c == col), 1.0, 0.0).astype(F32)
                value = value + term * weight
            acc[col, :, lo:hi] = value

    own_flag = jnp.zeros((), jnp.int32)
    for k in range(plan.shape[1]):
        own_flag = jnp.where(plan[mp, k] == own_block, 1, own_flag)
    own_flag = jnp.where(own_block < nblk, own_flag, 0)

    def new_left():
        nl[...] = BETA * nl[...] + dot_nt(gh[...], gh[...]) + dot_nt(gh[...], gl[...]) + dot_nt(gl[...], gh[...])

    def new_right():
        nr[...] = BETA * nr[...] + dot_tn(gh[...], gh[...]) + dot_tn(gh[...], gl[...]) + dot_tn(gl[...], gh[...])

    width = half

    def eye_tile(lo):
        rows = lax.broadcasted_iota(jnp.int32, (bs, width), 0)
        cols = lax.broadcasted_iota(jnp.int32, (bs, width), 1) + lo
        return jnp.where(rows == cols, 1.0, 0.0).astype(F32)

    def tiles(body):
        for lo in range(0, bs, width):
            body(slice(lo, lo + width), lo)

    def newton(stats, old):
        scale = {}

        def start():
            total = jnp.sum(stats[...] * stats[...], axis=(0, 1), keepdims=True)
            scale["z"] = 5.0 / (2.0 * jnp.sqrt(total + EPS))
            scale["root"] = jnp.sqrt(jnp.sqrt(scale["z"]))
            mb0[...] = (scale["z"] * stats[...]).astype(BF)

            def body(cols, lo):
                value = (-0.625 * scale["z"]) * stats[:, cols] + 0.0625 * dot(mb0[...], mb0[:, cols])
                nf[:, cols] = value
                nb[:, cols] = value.astype(BF)

            tiles(body)

        def fourth_power():
            def body(cols, lo):
                kb[:, cols] = (3.125 * nf[:, cols] + dot(nb[...], nb[:, cols])).astype(BF)

            tiles(body)

        def first_coupled():
            def body(cols, lo):
                value = (2.44140625 * scale["z"]) * stats[:, cols] + dot(kb[...], mb0[:, cols])
                m1f[:, cols] = value
                mb1[:, cols] = value.astype(BF)

            tiles(body)

        def second_iterate():
            def body(cols, lo):
                value = 1.5625 * eye_tile(lo) - 0.3125 * (scale["z"] * stats[:, cols] + m1f[:, cols])
                value = scale["root"] * (value + 0.0625 * dot(mb0[...], mb1[:, cols]))
                xf[:, cols] = value
                xb[:, cols] = value.astype(BF)

            tiles(body)

        def second_square():
            def body(cols, lo):
                value = -0.625 * m1f[:, cols] + 0.0625 * dot(mb1[...], mb1[:, cols])
                nf[:, cols] = value
                nb[:, cols] = value.astype(BF)

            tiles(body)

        def second_coupled():
            def body(cols, lo):
                mb0[:, cols] = (2.44140625 * m1f[:, cols] + dot(kb[...], mb1[:, cols])).astype(BF)

            tiles(body)

        def finish():
            mask = jnp.full((bs, width), own_flag, jnp.int32) > 0

            def body(cols, lo):
                value = 1.25 * xf[:, cols] - 0.25 * dot(xb[...], mb0[:, cols])
                old[:, cols] = jnp.where(mask, value, old[:, cols])

            tiles(body)

        return [start, fourth_power, first_coupled, second_iterate, second_square, fourth_power, second_coupled, finish]

    work = [new_left, new_right] + newton(nl, lold) + newton(nr, rold)

    def some(count):
        for _ in range(count):
            if work:
                work.pop(0)()

    def projection_part(p):
        other = pl.ds(pl.multiple_of((1 - y) * toks, toks), toks)
        ysends[p][...] = acc[:, other, chunks[p][0] : chunks[p][1]].astype(BF)
        return remote(ysends[p], yrecvs[p], y_ssem.at[p], y_rsem.at[p], across)

    def projection_end(p, copy):
        copy.wait_recv()
        own = pl.ds(pl.multiple_of(y * toks, toks), toks)
        lo, hi = chunks[p]
        value = acc[:, own, lo:hi] + yrecvs[p][...].astype(F32)
        for col in range(CB):
            pout[:, col * bs + lo : col * bs + hi] = value[col].astype(BF)

    y_copy = {}
    sib_steps = [1, 1]
    ready = []
    later = []

    def compute(count):
        for _ in range(count):
            if ready:
                ready.pop(0)()
            else:
                some(1)
        for entry in later:
            entry[0] -= 1
        while later and later[0][0] <= 0:
            ready.append(later.pop(0)[1])

    def sibling_products(p, items):
        for step, _ in items:
            sib[step, p].wait_recv()
        add_products(p, [(1 - core, zz) for _, zz in items])

    def finish_chunk(p):
        y_copy[p] = projection_part(p)

    def receive(p, d, k):
        for way in range(2):
            order = k if way == 0 else 1 - k
            if d <= reach(way, order):
                ag[way, d, p, order].wait_recv()
                if d < reach(way, order):
                    send_ring(way, behind(way, d), d + 1, p, order)
        if k == 1 or d == far:
            arrived = [behind(0, d), behind(1, d)] if d < far else [behind(0, d)]
            fresh = []
            for zz in arrived:
                send_sibling(zz, sib_steps[p], p)
                fresh.append((sib_steps[p], zz))
                sib_steps[p] += 1
            ready.append(functools.partial(add_products, p, [(core, zz) for zz in arrived]))
            later.append([SIBLING_LAG, functools.partial(sibling_products, p, fresh)])
            if d == far:
                later.append([SIBLING_LAG, functools.partial(finish_chunk, p)])

    make_weights(0)
    send_own(0, 0)
    send_own(0, 1)
    send_sibling(z, 0, 0)
    make_weights(1)
    send_own(1, 0)
    send_sibling(z, 0, 1)
    acc[...] = jnp.zeros_like(acc)
    ready.append(functools.partial(add_products, 0, [(core, z)]))
    later.append([SIBLING_LAG, functools.partial(sibling_products, 0, [(0, z)])])
    compute(2)
    for d in range(1, far + 1):
        for k in range(2 if d < far else 1):
            receive(0, d, k)
            if d == 1 and k == 1:
                send_own(1, 1)
            compute(PACE)
            if (d, k) == (max(far - 2, 1), 1):
                receive(1, 1, 0)
                ready.append(functools.partial(add_products, 1, [(core, z)]))
                later.append([SIBLING_LAG, functools.partial(sibling_products, 1, [(0, z)])])
                compute(PACE)
            if (d, k) == (far - 1, 1):
                receive(1, 1, 1)
                compute(PACE)
    for d in range(2, far + 1):
        for k in range(2 if d < far else 1):
            receive(1, d, k)
            compute(PACE if d < far else 1)
    ready.extend(entry[1] for entry in later)
    while ready:
        ready.pop(0)()
    some(len(work))
    for p in range(2):
        projection_end(p, y_copy[p])

    sent((4, 5))
    for group in (to_sibling, forwarded, rs_copy, ag, sib, y_copy):
        for copy in group.values():
            copy.wait_send()


def hand_over(*refs):
    count = (len(refs) - 1) // 2
    sems = refs[-1]
    copies = [pltpu.make_async_copy(refs[k], refs[count + k], sems.at[k]) for k in range(count)]
    for copy in copies:
        copy.start()
    for copy in copies:
        copy.wait()


def solution(mesh):
    zs = mesh.shape["dp"] // 4

    def on_device(act, og, table, plan, ls, rs, lr, rr, wb):
        toks = act.shape[0]
        bs = ls.shape[-1]
        rb = act.shape[1] // bs
        slots = table.shape[1]
        half = bs // 2
        quarter = bs // 4
        mats = [value.reshape(bs, bs) for value in (ls, rs, lr, rr, wb)]
        far = zs // 2
        leaves = [jax.ShapeDtypeStruct((bs, bs), F32)] * 4
        leaves += [jax.ShapeDtypeStruct((bs, bs), BF), jax.ShapeDtypeStruct((toks, CB * bs), BF)]
        vmem = pl.BlockSpec(memory_space=pltpu.VMEM)
        any_space = pl.BlockSpec(memory_space=pl.ANY)
        smem = pl.BlockSpec(memory_space=pltpu.SMEM)
        f_mat = pltpu.VMEM((bs, bs), F32)
        b_mat = pltpu.VMEM((bs, bs), BF)
        dma = pltpu.SemaphoreType.DMA
        outs = pl.pallas_call(
            functools.partial(kernel, zs, toks, rb, bs, slots),
            out_shape=[pltpu.VMEM(leaf.shape, leaf.dtype) for leaf in leaves],
            in_specs=[smem, smem] + [any_space] * 7,
            out_specs=[vmem] * 6,
            scratch_shapes=[
                pltpu.VMEM((rb, 4 * toks, quarter), BF),
                pltpu.VMEM((rb, 4 * toks, quarter), BF),
                pltpu.VMEM((rb, 4 * toks, half), BF),
                pltpu.VMEM((CB, 4 * toks, half), BF),
                pltpu.VMEM((CB, 4 * toks, half), BF),
                pltpu.VMEM((2, 2, half, half), BF),
                pltpu.VMEM((2, 2, half, half), BF),
                pltpu.VMEM((2, far - 1, 2, bs, half), BF),
                pltpu.VMEM((2, far - 1, 2, bs, half), BF),
                pltpu.VMEM((2, zs, bs, half), BF),
                pltpu.VMEM((2, zs, bs, half), BF),
                pltpu.VMEM((CB, 2 * toks, bs), F32),
                pltpu.VMEM((CB, toks, half), BF),
                pltpu.VMEM((CB, toks, half), BF),
                pltpu.VMEM((CB, toks, half), BF),
                pltpu.VMEM((CB, toks, half), BF),
                b_mat,
                pltpu.VMEM((2, 2, half, half), F32),
                b_mat, b_mat, b_mat, b_mat, b_mat, b_mat, b_mat, b_mat,
                pltpu.VMEM((bs, half), F32),
                f_mat, f_mat, f_mat, b_mat, b_mat, b_mat, b_mat, b_mat,
                pltpu.SemaphoreType.REGULAR,
                dma((2 * CB + 3 * rb + 5,)),
                dma((18,)), dma((18,)),
                dma((2, far + 1, 6)), dma((2, far + 1, 6)),
                dma((2, far, 2, 2)), dma((2, far, 2, 2)),
                dma((zs, 2)), dma((zs, 2)),
                dma((2,)), dma((2,)),
            ],
            compiler_params=pltpu.CompilerParams(
                collective_id=0, has_side_effects=True, vmem_limit_bytes=57 * 1024 * 1024
            ),
        )(table, plan, act, og, *mats)
        outs = pl.pallas_call(
            hand_over,
            out_shape=leaves,
            in_specs=[vmem] * 6,
            out_specs=[any_space] * 6,
            scratch_shapes=[dma((6,))],
            compiler_params=pltpu.CompilerParams(vmem_limit_bytes=4 * 1024 * 1024),
        )(*[pltpu.with_memory_space_constraint(value, pltpu.VMEM) for value in outs])
        return tuple(value.reshape(1, 1, bs, bs) for value in outs[:5]) + (outs[5],)

    block = P("mp", "dp", None, None)
    return jax.shard_map(
        on_device,
        mesh=mesh,
        in_specs=(P("dp", None), P("dp", "mp"), P(), P(), block, block, block, block, block),
        out_specs=(block, block, block, block, block, P("dp", "mp")),
        check_vma=False,
    )
```

```python
import functools

import jax
import jax.numpy as jnp
from jax import lax
from jax.experimental import pallas as pl
from jax.experimental.pallas import tpu as pltpu
from jax.sharding import PartitionSpec as P

BETA = 0.9
STEP = 0.1
EPS = 1e-06
CB = 4

PACE = 3
SIBLING_LAG = 2

MESH = pl.DeviceIdType.MESH
BF = jnp.bfloat16
F32 = jnp.float32


def dot(left, right):
    return jnp.dot(left, right, preferred_element_type=F32)


def dot_tn(left, right):
    return lax.dot_general(left, right, (((0,), (0,)), ((), ())), preferred_element_type=F32)


def dot_nt(left, right):
    return lax.dot_general(left, right, (((1,), (1,)), ((), ())), preferred_element_type=F32)


def split(value):
    high = value.astype(BF)
    return high, (value - high.astype(F32)).astype(BF)


def kernel(
    zs, toks, rb, bs, slots,
    table, plan, act, og, ls, rs, lr, rr, wb,
    nl, nr, lold, rold, nw, pout,
    a_0, a_1, a_2, e_0, e_1, far_s, far_r, near_s, near_r, wag_0, wag_1, acc, ysend_0, ysend_1, yrecv_0, yrecv_1,
    wold, mid, lh, ll, rh, rl, gh, gl, th, tl, tf,
    nf, m1f, xf, mb0, mb1, nb, kb, xb,
    gate, load_sem, p0_send, p0_recv, rs_send, rs_recv, ag_send, ag_recv, sib_send, sib_recv, y_ssem, y_rsem,
):
    half = bs // 2
    quarter = bs // 4
    far = zs // 2
    a_parts, e_parts = (a_0, a_1, a_2), (e_0, e_1)
    a_cols = ((0, quarter), (quarter, half), (half, bs))
    wags, ysends, yrecvs = (wag_0, wag_1), (ysend_0, ysend_1), (yrecv_0, yrecv_1)
    chunks = ((0, half), (half, bs))
    nblk = rb * CB
    dp = lax.axis_index("dp")
    mp = lax.axis_index("mp")
    core = lax.rem(dp, 2)
    z = lax.rem(dp // 2, zs)
    y = dp // (2 * zs)

    def device(yy, zz, cc):
        return yy * (2 * zs) + zz * 2 + cc

    up = lax.rem(z + 1, zs)
    down = lax.rem(z + zs - 1, zs)
    ring = ((device(y, up, core), mp), (device(y, down, core), mp))
    sibling = (device(y, z, 1 - core), mp)
    across = (device(1 - y, z, core), mp)
    across_other = (device(1 - y, z, core), mp + 1 - 2 * lax.rem(mp, 2))

    def remote(src, dst, send, recv, to):
        copy = pltpu.make_async_remote_copy(
            src_ref=src, dst_ref=dst, send_sem=send, recv_sem=recv, device_id=to, device_id_type=MESH
        )
        copy.start()
        return copy

    def rows_of(yy, cc):
        return pl.ds(pl.multiple_of((cc * 2 + yy) * toks, toks), toks)

    def local(src, dst, sem):
        copy = pltpu.make_async_copy(src, dst, sem)
        copy.start()
        return copy

    mine = rows_of(y, core)
    loads = {}
    base = 0
    for kind, i in (("e", 0), ("a", 0), ("a", 1), ("e", 1), ("a", 2)):
        source, dst, count = (og, e_parts[i], CB) if kind == "e" else (act, a_parts[i], rb)
        lo, hi = (i * half, (i + 1) * half) if kind == "e" else a_cols[i]
        loads[kind, i] = [
            local(source.at[:, k * bs + lo : k * bs + hi], dst.at[k, mine, :], load_sem.at[base + k]) for k in range(count)
        ]
        base += count
    load_mats = [
        local(src, dst, load_sem.at[base + k])
        for k, (src, dst) in enumerate(((lr, lold), (rr, rold), (wb, wold), (ls, nl), (rs, nr)))
    ]

    barrier = pltpu.get_barrier_semaphore()
    for other in (sibling, across, across_other) + ring:
        pl.semaphore_signal(barrier, inc=1, device_id=other, device_id_type=MESH)
    pl.semaphore_wait(barrier, 5)

    def part(number, rows):
        return (
            e_0.at[:, rows, :],
            a_0.at[:, rows, :],
            e_1.at[:, rows, :],
            a_1.at[:, rows, :],
            a_2.at[rb - 2 : rb, rows, :],
            a_2.at[0 : rb - 2, rows, :],
        )[number]

    parts = 6

    def send_part(number, rows, slot, to):
        ref = part(number, rows)
        return remote(ref, ref, p0_send.at[slot], p0_recv.at[slot], to)

    outgoing = {}
    to_sibling = {}
    forwarded = {}

    def send_parts(numbers, needs):
        for what in needs:
            for copy in loads[what]:
                copy.wait()
        for number in numbers:
            outgoing[number] = send_part(number, mine, number, across_other if number in (1, 3, 5) else across)
        for number in numbers:
            to_sibling[number] = send_part(number, mine, parts + number, sibling)

    def sent(numbers):
        for number in numbers:
            outgoing[number].wait_send()

    send_parts((0, 1), (("e", 0), ("a", 0)))
    sent((0, 1))
    send_parts((2, 3), (("e", 1), ("a", 1)))
    sent((2, 3))
    send_parts((4, 5), (("a", 2),))
    theirs = rows_of(1 - y, core)

    def forward(numbers):
        for number in numbers:
            outgoing[number].wait_recv()
            forwarded[number] = send_part(number, theirs, 2 * parts + number, sibling)

    def have(numbers):
        for number in numbers:
            to_sibling[number].wait_recv()
            forwarded[number].wait_recv()

    def block_at(zz, cc):
        return table[mp, y * (2 * zs) + zz * 2 + cc]

    def row_and_col(block):
        safe = jnp.where(block < nblk, block, 0)
        return safe // CB, lax.rem(safe, CB)

    def partial_grad(zz, piece):
        r, c = row_and_col(block_at(zz, core))
        return dot_tn(a_parts[piece[0]][r], e_parts[piece[1]][c])

    pieces = ((0, 0), (1, 0), (0, 1), (1, 1), (2, 0), (2, 1))
    rs_copy = {}

    def piece_rows(piece, part=None):
        lo, hi = a_cols[piece[0]]
        if part is None:
            return slice(lo, hi)
        middle = (lo + hi) // 2
        return slice(lo, middle) if part == 0 else slice(middle, hi)

    def send_sum(way, level, piece, src, dst):
        n = pieces.index(piece)
        rs_copy[way, level, piece] = remote(src, dst, rs_send.at[way, level, n], rs_recv.at[way, level, n], ring[way])

    def target(way, d):
        return lax.rem(z + d, zs) if way == 0 else lax.rem(z + zs - d, zs)

    def send_start(piece):
        j = piece[1]
        lo, hi = a_cols[piece[0]]
        middle = (hi - lo) // 2
        rows = slice(lo // 2, hi // 2)
        value = partial_grad(target(0, far), piece).astype(BF)
        for way in range(2):
            far_s[way, j, rows, :] = value[way * middle : (way + 1) * middle, :]
            send_sum(way, 0, piece, far_s.at[way, j, rows, :], far_r.at[way, j, rows, :])
        for way in range(2):
            rest = 1 - way
            value = partial_grad(target(way, far - 1), piece)
            rows = piece_rows(piece, rest)
            near_s[way, far - 2, j, rows, :] = value[rest * middle : (rest + 1) * middle, :].astype(BF)
            mid[way, j, lo // 2 : hi // 2, :] = value[way * middle : (way + 1) * middle, :]
            send_sum(way, far, piece, near_s.at[way, far - 2, j, rows, :], near_r.at[way, far - 2, j, rows, :])

    def send_near(d, piece):
        if d < 1:
            return
        j = piece[1]
        lo, hi = a_cols[piece[0]]
        for way in range(2):
            if d == far - 1:
                rows = piece_rows(piece, way)
                value = mid[way, j, lo // 2 : hi // 2, :]
                rs_copy[way, 0, piece].wait_recv()
                value = value + far_r[way, j, lo // 2 : hi // 2, :].astype(F32)
            else:
                rows = piece_rows(piece)
                value = partial_grad(target(way, d), piece)
                rs_copy[way, d + 1, piece].wait_recv()
                if d == far - 2:
                    rs_copy[way, far, piece].wait_recv()
                value = value + near_r[way, d, j, rows, :].astype(F32)
            near_s[way, d - 1, j, rows, :] = value.astype(BF)
            send_sum(way, d, piece, near_s.at[way, d - 1, j, rows, :], near_r.at[way, d - 1, j, rows, :])

    forward((0, 1))
    have((0, 1))
    send_start(pieces[0])
    forward((3,))
    have((3,))
    send_start(pieces[1])
    forward((2,))
    send_near(far - 1, pieces[0])
    have((2,))
    send_start(pieces[2])
    send_start(pieces[3])
    send_near(far - 1, pieces[1])
    send_near(far - 2, pieces[0])
    forward((4, 5))
    have((4, 5))
    send_start(pieces[4])
    send_start(pieces[5])
    send_near(far - 1, pieces[2])
    send_near(far - 1, pieces[3])
    send_near(far - 2, pieces[1])
    send_near(far - 1, pieces[4])
    send_near(far - 1, pieces[5])
    send_near(far - 2, pieces[2])
    send_near(far - 2, pieces[3])
    for copy in load_mats:
        copy.wait()
    lh[...], ll[...] = split(lold[...])
    rh[...], rl[...] = split(rold[...])
    send_near(far - 3, pieces[0])
    send_near(far - 3, pieces[1])

    @pl.when(core == 1)
    def _():
        pl.semaphore_wait(gate, 1)

    send_near(far - 2, pieces[4])
    send_near(far - 2, pieces[5])
    send_near(far - 3, pieces[2])
    send_near(far - 3, pieces[3])
    send_near(far - 3, pieces[4])
    send_near(far - 3, pieces[5])

    @pl.when(core == 0)
    def _():
        pl.semaphore_signal(gate, inc=1, device_id=sibling, device_id_type=MESH)

    own_block = block_at(z, core)
    filled = jnp.where(own_block < nblk, 1.0, 0.0).astype(F32)

    def sum_piece(piece):
        j = piece[1]
        rows = piece_rows(piece)
        cols = slice(j * half, (j + 1) * half)
        value = partial_grad(z, piece)
        for way in range(2):
            rs_copy[way, 1, piece].wait_recv()
            if far == 2:
                rs_copy[way, far, piece].wait_recv()
        value = (value + near_r[0, 0, j, rows, :].astype(F32) + near_r[1, 0, j, rows, :].astype(F32)) * filled
        gh[rows, cols], gl[rows, cols] = split(value)

    def left_term(i, j):
        rows, cols = slice(i * half, (i + 1) * half), slice(j * half, (j + 1) * half)
        return dot(lh[:, rows], gh[rows, cols]) + dot(lh[:, rows], gl[rows, cols]) + dot(ll[:, rows], gh[rows, cols])

    def right_term(j, lo, hi):
        rows = slice(j * half, (j + 1) * half)
        return dot(th[:, rows], rh[rows, lo:hi]) + dot(th[:, rows], rl[rows, lo:hi]) + dot(tl[:, rows], rh[rows, lo:hi])

    lefts = []
    for j in range(2):
        sum_piece((0, j))
        sum_piece((1, j))
        lefts.append(left_term(0, j))
    for j in range(2):
        sum_piece((2, j))
        cols = slice(j * half, (j + 1) * half)
        th[:, cols], tl[:, cols] = split(lefts[j] + left_term(1, j))
        if j == 0:
            tf[...] = right_term(0, *chunks[0])

    ag = {}
    sib = {}

    def piece(cc, zz, p, k):
        return wags[p].at[cc, zz, k * half : (k + 1) * half, :]

    def send_ring(way, zz, d, p, k):
        ref = piece(core, zz, p, k)
        ag[way, d, p, k] = remote(ref, ref, ag_send.at[way, d - 1, p, k], ag_recv.at[way, d - 1, p, k], ring[way])

    def send_sibling(zz, step, p):
        ref = wags[p].at[core, zz]
        sib[step, p] = remote(ref, ref, sib_send.at[step, p], sib_recv.at[step, p], sibling)

    def reach(way, k):
        return far if way == k else far - 1

    def behind(way, d):
        return lax.rem(z + zs - d, zs) if way == 0 else lax.rem(z + d, zs)

    def make_weights(p):
        lo, hi = chunks[p]
        update = (tf[...] if p == 0 else right_term(0, lo, hi)) + right_term(1, lo, hi)
        value = (wold[:, lo:hi].astype(F32) - STEP * update).astype(BF)
        wags[p][core, z] = value
        nw[:, lo:hi] = value

    def send_own(p, k):
        for way in range(2):
            send_ring(way, z, 1, p, k if way == 0 else 1 - k)

    def add_products(p, items):
        lo, hi = chunks[p]
        terms = []
        for cc, zz in items:
            block = block_at(zz, cc)
            r, c = row_and_col(block)
            rows = pl.ds(pl.multiple_of(core * (2 * toks), 2 * toks), 2 * toks)
            lhs = jnp.concatenate([a_0[r, rows, :], a_1[r, rows, :]], axis=1)
            term = dot(lhs, wags[p][cc, zz, 0:half, :]) + dot(a_2[r, rows, :], wags[p][cc, zz, half:bs, :])
            terms.append((block, c, term))
        for col in range(CB):
            value = acc[col, :, lo:hi]
            for block, c, term in terms:
                weight = jnp.where((block < nblk) & (c == col), 1.0, 0.0).astype(F32)
                value = value + term * weight
            acc[col, :, lo:hi] = value

    own_flag = jnp.zeros((), jnp.int32)
    for k in range(plan.shape[1]):
        own_flag = jnp.where(plan[mp, k] == own_block, 1, own_flag)
    own_flag = jnp.where(own_block < nblk, own_flag, 0)

    def new_left():
        nl[...] = BETA * nl[...] + dot_nt(gh[...], gh[...]) + dot_nt(gh[...], gl[...]) + dot_nt(gl[...], gh[...])

    def new_right():
        nr[...] = BETA * nr[...] + dot_tn(gh[...], gh[...]) + dot_tn(gh[...], gl[...]) + dot_tn(gl[...], gh[...])

    width = half

    def eye_tile(lo):
        rows = lax.broadcasted_iota(jnp.int32, (bs, width), 0)
        cols = lax.broadcasted_iota(jnp.int32, (bs, width), 1) + lo
        return jnp.where(rows == cols, 1.0, 0.0).astype(F32)

    def tiles(body):
        for lo in range(0, bs, width):
            body(slice(lo, lo + width), lo)

    def newton(stats, old):
        scale = {}

        def start():
            total = jnp.sum(stats[...] * stats[...], axis=(0, 1), keepdims=True)
            scale["z"] = 5.0 / (2.0 * jnp.sqrt(total + EPS))
            scale["root"] = jnp.sqrt(jnp.sqrt(scale["z"]))
            mb0[...] = (scale["z"] * stats[...]).astype(BF)

            def body(cols, lo):
                value = (-0.625 * scale["z"]) * stats[:, cols] + 0.0625 * dot(mb0[...], mb0[:, cols])
                nf[:, cols] = value
                nb[:, cols] = value.astype(BF)

            tiles(body)

        def fourth_power():
            def body(cols, lo):
                kb[:, cols] = (3.125 * nf[:, cols] + dot(nb[...], nb[:, cols])).astype(BF)

            tiles(body)

        def first_coupled():
            def body(cols, lo):
                value = (2.44140625 * scale["z"]) * stats[:, cols] + dot(kb[...], mb0[:, cols])
                m1f[:, cols] = value
                mb1[:, cols] = value.astype(BF)

            tiles(body)

        def second_iterate():
            def body(cols, lo):
                value = 1.5625 * eye_tile(lo) - 0.3125 * (scale["z"] * stats[:, cols] + m1f[:, cols])
                value = scale["root"] * (value + 0.0625 * dot(mb0[...], mb1[:, cols]))
                xf[:, cols] = value
                xb[:, cols] = value.astype(BF)

            tiles(body)

        def second_square():
            def body(cols, lo):
                value = -0.625 * m1f[:, cols] + 0.0625 * dot(mb1[...], mb1[:, cols])
                nf[:, cols] = value
                nb[:, cols] = value.astype(BF)

            tiles(body)

        def second_coupled():
            def body(cols, lo):
                mb0[:, cols] = (2.44140625 * m1f[:, cols] + dot(kb[...], mb1[:, cols])).astype(BF)

            tiles(body)

        def finish():
            mask = jnp.full((bs, width), own_flag, jnp.int32) > 0

            def body(cols, lo):
                value = 1.25 * xf[:, cols] - 0.25 * dot(xb[...], mb0[:, cols])
                old[:, cols] = jnp.where(mask, value, old[:, cols])

            tiles(body)

        return [start, fourth_power, first_coupled, second_iterate, second_square, fourth_power, second_coupled, finish]

    work = [new_left, new_right] + newton(nl, lold) + newton(nr, rold)

    def some(count):
        for _ in range(count):
            if work:
                work.pop(0)()

    def projection_part(p):
        other = pl.ds(pl.multiple_of((1 - y) * toks, toks), toks)
        ysends[p][...] = acc[:, other, chunks[p][0] : chunks[p][1]].astype(BF)
        return remote(ysends[p], yrecvs[p], y_ssem.at[p], y_rsem.at[p], across)

    def projection_end(p, copy):
        copy.wait_recv()
        own = pl.ds(pl.multiple_of(y * toks, toks), toks)
        lo, hi = chunks[p]
        value = acc[:, own, lo:hi] + yrecvs[p][...].astype(F32)
        for col in range(CB):
            pout[:, col * bs + lo : col * bs + hi] = value[col].astype(BF)

    y_copy = {}
    sib_steps = [1, 1]
    ready = []
    later = []

    def compute(count):
        for _ in range(count):
            if ready:
                ready.pop(0)()
            else:
                some(1)
        for entry in later:
            entry[0] -= 1
        while later and later[0][0] <= 0:
            ready.append(later.pop(0)[1])

    def sibling_products(p, items):
        for step, _ in items:
            sib[step, p].wait_recv()
        add_products(p, [(1 - core, zz) for _, zz in items])

    def finish_chunk(p):
        y_copy[p] = projection_part(p)

    def receive(p, d, k):
        for way in range(2):
            order = k if way == 0 else 1 - k
            if d <= reach(way, order):
                ag[way, d, p, order].wait_recv()
                if d < reach(way, order):
                    send_ring(way, behind(way, d), d + 1, p, order)
        if k == 1 or d == far:
            arrived = [behind(0, d), behind(1, d)] if d < far else [behind(0, d)]
            fresh = []
            for zz in arrived:
                send_sibling(zz, sib_steps[p], p)
                fresh.append((sib_steps[p], zz))
                sib_steps[p] += 1
            ready.append(functools.partial(add_products, p, [(core, zz) for zz in arrived]))
            later.append([SIBLING_LAG, functools.partial(sibling_products, p, fresh)])
            if d == far:
                later.append([SIBLING_LAG, functools.partial(finish_chunk, p)])

    make_weights(0)
    send_own(0, 0)
    send_own(0, 1)
    send_sibling(z, 0, 0)
    make_weights(1)
    send_own(1, 0)
    send_sibling(z, 0, 1)
    acc[...] = jnp.zeros_like(acc)
    ready.append(functools.partial(add_products, 0, [(core, z)]))
    later.append([SIBLING_LAG, functools.partial(sibling_products, 0, [(0, z)])])
    compute(2)
    for d in range(1, far + 1):
        for k in range(2 if d < far else 1):
            receive(0, d, k)
            if d == 1 and k == 1:
                send_own(1, 1)
            compute(PACE)
            if (d, k) == (max(far - 2, 1), 1):
                receive(1, 1, 0)
                ready.append(functools.partial(add_products, 1, [(core, z)]))
                later.append([SIBLING_LAG, functools.partial(sibling_products, 1, [(0, z)])])
                compute(PACE)
            if (d, k) == (far - 1, 1):
                receive(1, 1, 1)
                compute(PACE)
    for d in range(2, far + 1):
        for k in range(2 if d < far else 1):
            receive(1, d, k)
            compute(PACE if d < far else 1)
    ready.extend(entry[1] for entry in later)
    while ready:
        ready.pop(0)()
    some(len(work))
    for p in range(2):
        projection_end(p, y_copy[p])

    sent((4, 5))
    for group in (to_sibling, forwarded, rs_copy, ag, sib, y_copy):
        for copy in group.values():
            copy.wait_send()


def hand_over(*refs):
    count = (len(refs) - 1) // 2
    sems = refs[-1]
    copies = [pltpu.make_async_copy(refs[k], refs[count + k], sems.at[k]) for k in range(count)]
    for copy in copies:
        copy.start()
    for copy in copies:
        copy.wait()


def solution(mesh):
    zs = mesh.shape["dp"] // 4

    def on_device(act, og, table, plan, ls, rs, lr, rr, wb):
        toks = act.shape[0]
        bs = ls.shape[-1]
        rb = act.shape[1] // bs
        slots = table.shape[1]
        half = bs // 2
        quarter = bs // 4
        mats = [value.reshape(bs, bs) for value in (ls, rs, lr, rr, wb)]
        far = zs // 2
        leaves = [jax.ShapeDtypeStruct((bs, bs), F32)] * 4
        leaves += [jax.ShapeDtypeStruct((bs, bs), BF), jax.ShapeDtypeStruct((toks, CB * bs), BF)]
        vmem = pl.BlockSpec(memory_space=pltpu.VMEM)
        any_space = pl.BlockSpec(memory_space=pl.ANY)
        smem = pl.BlockSpec(memory_space=pltpu.SMEM)
        f_mat = pltpu.VMEM((bs, bs), F32)
        b_mat = pltpu.VMEM((bs, bs), BF)
        dma = pltpu.SemaphoreType.DMA
        outs = pl.pallas_call(
            functools.partial(kernel, zs, toks, rb, bs, slots),
            out_shape=[pltpu.VMEM(leaf.shape, leaf.dtype) for leaf in leaves],
            in_specs=[smem, smem] + [any_space] * 7,
            out_specs=[vmem] * 6,
            scratch_shapes=[
                pltpu.VMEM((rb, 4 * toks, quarter), BF),
                pltpu.VMEM((rb, 4 * toks, quarter), BF),
                pltpu.VMEM((rb, 4 * toks, half), BF),
                pltpu.VMEM((CB, 4 * toks, half), BF),
                pltpu.VMEM((CB, 4 * toks, half), BF),
                pltpu.VMEM((2, 2, half, half), BF),
                pltpu.VMEM((2, 2, half, half), BF),
                pltpu.VMEM((2, far - 1, 2, bs, half), BF),
                pltpu.VMEM((2, far - 1, 2, bs, half), BF),
                pltpu.VMEM((2, zs, bs, half), BF),
                pltpu.VMEM((2, zs, bs, half), BF),
                pltpu.VMEM((CB, 2 * toks, bs), F32),
                pltpu.VMEM((CB, toks, half), BF),
                pltpu.VMEM((CB, toks, half), BF),
                pltpu.VMEM((CB, toks, half), BF),
                pltpu.VMEM((CB, toks, half), BF),
                b_mat,
                pltpu.VMEM((2, 2, half, half), F32),
                b_mat, b_mat, b_mat, b_mat, b_mat, b_mat, b_mat, b_mat,
                pltpu.VMEM((bs, half), F32),
                f_mat, f_mat, f_mat, b_mat, b_mat, b_mat, b_mat, b_mat,
                pltpu.SemaphoreType.REGULAR,
                dma((2 * CB + 3 * rb + 5,)),
                dma((18,)), dma((18,)),
                dma((2, far + 1, 6)), dma((2, far + 1, 6)),
                dma((2, far, 2, 2)), dma((2, far, 2, 2)),
                dma((zs, 2)), dma((zs, 2)),
                dma((2,)), dma((2,)),
            ],
            compiler_params=pltpu.CompilerParams(
                collective_id=0, has_side_effects=True, vmem_limit_bytes=57 * 1024 * 1024
            ),
        )(table, plan, act, og, *mats)
        outs = pl.pallas_call(
            hand_over,
            out_shape=leaves,
            in_specs=[vmem] * 6,
            out_specs=[any_space] * 6,
            scratch_shapes=[dma((6,))],
            compiler_params=pltpu.CompilerParams(vmem_limit_bytes=4 * 1024 * 1024),
        )(*[pltpu.with_memory_space_constraint(value, pltpu.VMEM) for value in outs])
        return tuple(value.reshape(1, 1, bs, bs) for value in outs[:5]) + (outs[5],)

    block = P("mp", "dp", None, None)
    return jax.shard_map(
        on_device,
        mesh=mesh,
        in_specs=(P("dp", None), P("dp", "mp"), P(), P(), block, block, block, block, block),
        out_specs=(block, block, block, block, block, P("dp", "mp")),
        check_vma=False,
    )
```
